32 devices in a mesh: px: 8 (over z, y), py: 4 (over x, core).
Axes of the slice: x: 2, y: 2, z: 4, core: 2. Of those that a mesh axis runs over, the one named last changes fastest.
Arguments:
- eta_boxes: float32 [128, 32, 32, 128], P(('px', 'py')), may hold values from 0 to 1
- corners: int32 [128, 2], P(('px', 'py')), may hold values from 0 to 95, as said below
- grain_ids: int32 [128], P(('px', 'py')), may hold values from 0 to 23
- misfit: float32 [24], replicated, may hold values from -1 to 1
- green: float32 [128, 768, 512], P('px', 'py'), may hold values from 0.25 to 2.5
Outputs:
- eta_next: float32 [128, 32, 32, 128], P(('px', 'py'))
- potential: float32 [768, 512, 128], P('px', 'py')
The draws below stay inside these ranges and needn't reach their ends.
Inputs may be any that keep to these rules, and one draw needn't show every extreme that they name: Box b lies with device d = b // 4 (px index p = d // 4, py index q = d % 4): 8 corners[b,0] lies in [p * 96, (p + 1) * 96) and 8 corners[b,1] in [q * 128, (q + 1) * 128). Among each device's boxes one has its corner at the last tile grid position of that device's cells in both columns.
All inputs are finite; a program needn't handle non-finite values.
Results may differ from the reference program's by a relative error of at most 0.000075.
Values sent between devices are 32-bit elements; how exact they have to be, the bound alone decides.
No kernel may reach another device: no remote copies, remote signals or barrier semaphores. Data moves between devices by JAX's collectives and lax.ppermute only.
A program may use at most 192 MiB of HBM per device.

```python
import math
import jax
import jax.numpy as jnp
from jax import lax

NX = 768
NY = 512
NZ = 128
BX = 32
BY = 32
STEP = 8
VARIANTS = 24
BOX_DEV = 4
CX = 96
CY = 128
BOXES = 128


def draw_corners(key, part):
    owner = jnp.arange(BOXES, dtype=jnp.int32) // BOX_DEV
    slot_index = jnp.arange(BOXES, dtype=jnp.int32) % BOX_DEV
    devices_y = NY // CY
    row_dev = owner // devices_y
    col_dev = owner % devices_y
    steps_x = CX // STEP
    steps_y = CY // STEP
    first_key = jax.random.fold_in(key, 11)
    second_key = jax.random.fold_in(key, 12)
    third_key = jax.random.fold_in(key, 13)
    offset_x = jax.random.randint(first_key, (BOXES,), 0, steps_x, dtype=jnp.int32)
    offset_y = jax.random.randint(second_key, (BOXES,), 0, steps_y, dtype=jnp.int32)
    chosen = jax.random.randint(third_key, (BOXES // BOX_DEV,), 0, BOX_DEV, dtype=jnp.int32)
    forced = slot_index == chosen[owner]
    offset_x = jnp.where(forced, steps_x - 1, offset_x)
    offset_y = jnp.where(forced, steps_y - 1, offset_y)
    corner_x = row_dev * steps_x + offset_x
    corner_y = col_dev * steps_y + offset_y
    return jnp.stack([corner_x, corner_y], axis=1).astype(jnp.int32)


def with_ends(array, key, low, largest):
    index_at = [jax.random.randint(jax.random.fold_in(key, axis), (), 0, length) for axis, length in enumerate(array.shape)]
    main_axis = array.shape.index(max(array.shape))
    beside = index_at[:main_axis] + [(index_at[main_axis] + 1) % array.shape[main_axis]] + index_at[main_axis + 1:]
    return array.at[tuple(index_at)].set(low).at[tuple(beside)].set(largest)


def levels(stream_key, extent, cuts, least, largest):
    gain, own = 1.0, jax.random.fold_in(stream_key, 6)
    for dim, parts in cuts:
        heights = jnp.exp(jax.random.uniform(jax.random.fold_in(own, dim), (parts,), jnp.float32, least / len(cuts), largest / len(cuts)))
        gain = gain * jnp.repeat(heights, extent[dim] // parts).reshape([-1 if axis == dim else 1 for axis in range(len(extent))])
    return gain


def setup_inputs(seed: int = 0) -> dict:
    key_of = jax.random.split(jax.random.key(seed), 6)
    return {
        "eta_boxes": jnp.clip(1.0 * jax.random.uniform(key_of[0], (BOXES, BX, BY, NZ), jnp.float32) ** levels(key_of[0], (BOXES, BX, BY, NZ), ((0, 32),), -0.2, 0.2), 0.0, 1.0),
        "corners": draw_corners(jax.random.fold_in(key_of[5], 71), 0),
        "grain_ids": with_ends(jax.random.randint(key_of[2], (BOXES,), 0, VARIANTS), jax.random.fold_in(key_of[2], 1), 0, VARIANTS - 1).astype(jnp.int32),
        "misfit": jnp.clip(jax.random.uniform(key_of[3], (VARIANTS,), jnp.float32, -1.0, 1.0), -1.0, 1.0),
        "green": jnp.clip(jnp.exp(math.log(2.5) - 2.3025851 * jax.random.uniform(key_of[4], (NZ, NX, NY), jnp.float32) ** levels(key_of[4], (NZ, NX, NY), ((0, 8), (1, 4)), -0.2, 0.2)), 0.25, 2.5),
    }


rate_step = 0.2
gradient_coef = 0.1
coupling = 1.5


def laplace(values):
    padded = jnp.pad(values, ((1, 1), (1, 1), (0, 0)))
    beside_all = padded[2:, 1:-1] + padded[:-2, 1:-1] + padded[1:-1, 2:] + padded[1:-1, :-2]
    beside_all = beside_all + jnp.roll(values, 1, axis=2) + jnp.roll(values, -1, axis=2)
    return beside_all - 6.0 * values


def advance(order_param, weight, field_mu, occupancy):
    square = order_param * order_param
    force = order_param * square - order_param + 2.0 * coupling * order_param * (occupancy - square)
    force = force - gradient_coef * laplace(order_param) + 2.0 * weight * order_param * field_mu
    return order_param - rate_step * force


def reference(eta_boxes, corners, grain_ids, misfit, green):
    weights = misfit[grain_ids]
    squares = eta_boxes * eta_boxes
    starts = (corners * STEP).astype(jnp.int32)
    anchor_zero = jnp.zeros((), jnp.int32)
    canvas = jnp.zeros((2, NX + BX, NY + BY, NZ), jnp.float32)

    def place(running, inputs):
        square, weight, anchor = inputs
        contrib = jnp.stack([weight * square, square])
        position = (anchor_zero, anchor[0], anchor[1], anchor_zero)
        current = lax.dynamic_slice(running, position, contrib.shape)
        return lax.dynamic_update_slice(running, current + contrib, position), None

    canvas, unused = lax.scan(place, canvas, (squares, weights, starts))
    folded = canvas[:, :NX, :NY]
    folded = folded.at[:, :BX].add(canvas[:, NX:, :NY])
    folded = folded.at[:, :, :BY].add(canvas[:, :NX, NY:])
    folded = folded.at[:, :BX, :BY].add(canvas[:, NX:, NY:])
    multiplier = jnp.transpose(green, (1, 2, 0))
    spectrum = jnp.fft.fftn(folded[0]) * multiplier
    potential = jnp.real(jnp.fft.ifftn(spectrum)).astype(jnp.float32)
    stacked = jnp.stack([potential, folded[1]])
    wrapped = jnp.pad(stacked, ((0, 0), (0, BX), (0, BY), (0, 0)), mode="wrap")

    def update(inputs):
        order_param, weight, anchor = inputs
        position = (anchor_zero, anchor[0], anchor[1], anchor_zero)
        window_vals = lax.dynamic_slice(wrapped, position, (2, BX, BY, NZ))
        return advance(order_param, weight, window_vals[0], window_vals[1])

    eta_next = lax.map(update, (eta_boxes, weights, starts))
    return eta_next, potential
```

```python
import functools
import math

import jax
import jax.numpy as jnp
import ml_dtypes
import numpy as np
from jax import lax
from jax.experimental import pallas as pl
from jax.experimental.pallas import tpu as pltpu
from jax.sharding import PartitionSpec as P

STEP = 8
LANES = 128
RADIX = 3

rate_step = 0.2
gradient_coef = 0.1
coupling = 1.5

F32 = jnp.float32
BF16 = jnp.bfloat16
MIB = 1 << 20


def from_behind(shard, axis, by):
    peers = lax.axis_size(axis)
    return lax.ppermute(shard, axis, [(i, (i + by) % peers) for i in range(peers)])


def laplace(values):
    padded = jnp.pad(values, ((1, 1), (1, 1), (0, 0)))
    beside_all = padded[2:, 1:-1] + padded[:-2, 1:-1] + padded[1:-1, 2:] + padded[1:-1, :-2]
    beside_all = beside_all + jnp.roll(values, 1, axis=2) + jnp.roll(values, -1, axis=2)
    return beside_all - 6.0 * values


def advance(order_param, weight, field_mu, occupancy):
    square = order_param * order_param
    force = order_param * square - order_param + 2.0 * coupling * order_param * (occupancy - square)
    force = force - gradient_coef * laplace(order_param) + 2.0 * weight * order_param * field_mu
    return order_param - rate_step * force


def pair_of(table):
    high = table.astype(ml_dtypes.bfloat16)
    low = (table - high.astype(np.float64)).astype(ml_dtypes.bfloat16)
    return high, low


def angle_of(index, length):
    return (index % length) * (2.0 * math.pi / length)


def plane_frequencies(depth, owners):
    own = depth // owners
    half = own // 2
    return [[own * p + t + (1 if p < owners // 2 else 0) for t in range(half)] for p in range(owners)]


def depth_tables(depth, owners, scale):
    freqs = plane_frequencies(depth, owners)
    z = np.arange(depth)
    forward, inverse = [], []
    for p in range(owners):
        real, imag, real_inv, imag_inv = [], [], [], []
        for t, freq in enumerate(freqs[p]):
            angles = angle_of(freq * z, depth)
            if p == owners // 2 and t == 0:
                real.append(np.cos(angles))
                imag.append(np.ones(depth))
                real_inv.append(0.5 * scale * np.cos(angles))
                imag_inv.append(np.full(depth, 0.5 * scale))
            else:
                real.append(np.cos(angles))
                imag.append(-np.sin(angles))
                real_inv.append(scale * np.cos(angles))
                imag_inv.append(-scale * np.sin(angles))
        forward += real + imag
        inverse += real_inv + imag_inv
    return pair_of(np.array(forward)), pair_of(np.array(inverse))


def row_tables(length):
    part = length // RADIX
    m = np.arange(part)
    forward, inverse = [], []
    for l in range(RADIX):
        angles = angle_of(m[:, None] * (RADIX * m[None, :] + l), length)
        c, s = np.cos(angles), np.sin(angles)
        forward.append(np.block([[c, s], [-s, c]]))
        c, s = c.T, s.T
        inverse.append(np.block([[c, -s], [s, c]]))
    return pair_of(np.array(forward)), pair_of(np.array(inverse))


def column_tables(length):
    part = length // 2
    m = np.arange(part)
    forward, inverse = [], []
    for parity in range(2):
        angles = angle_of(m[:, None] * (2 * m[None, :] + parity), length)
        c, s = np.cos(angles), np.sin(angles)
        forward.append(np.block([[c, -s], [s, c]]))
        c, s = c.T, s.T
        inverse.append(np.block([[c, s], [-s, c]]))
    return pair_of(np.array(forward)), pair_of(np.array(inverse))


def mirror_tables(rows, length):
    part = length // 2
    m = np.arange(part)
    order = np.concatenate([2 * m, 2 * m + 1])
    straight = np.zeros((length, length))
    straight[order, np.arange(length)] = 1.0
    mirrored = np.zeros((length, length))
    mirrored[(length - order) % length, np.arange(length)] = 1.0
    flip = np.zeros((rows, rows))
    i = np.arange(1, rows)
    flip[i, rows - i] = 1.0
    as_bf16 = lambda table: table.astype(ml_dtypes.bfloat16)
    return as_bf16(straight), as_bf16(mirrored), as_bf16(flip)


def halves(values):
    high = values.astype(BF16)
    return high, (values - high.astype(F32)).astype(BF16)


def dot(a, b):
    return jnp.dot(a, b, preferred_element_type=F32)


def table_first(high, low, values):
    top, rest = halves(values)
    width = values.shape[1]
    if width % LANES == 0:
        both = dot(high, jnp.concatenate([top, rest], axis=1))
        both = both[:, :width] + both[:, width:]
    else:
        both = dot(high, top) + dot(high, rest)
    return both + dot(low, top)


def table_last(values, high, low):
    top, rest = halves(values)
    rows = values.shape[0]
    both = dot(jnp.concatenate([top, rest], axis=0), high)
    return both[:rows] + both[rows:] + dot(top, low)


def params(mib):
    return pltpu.CompilerParams(vmem_limit_bytes=mib * MIB)


def whole(array):
    rank = len(array.shape)
    return pl.BlockSpec(array.shape, lambda *_: (0,) * rank)


def depth_kernel(weights, eta, high, low, out):
    boxes, extent = eta.shape[0], eta.shape[1]
    planes = high.shape[0]
    for i in range(extent):
        rows = []
        for b in range(boxes):
            values = eta[b, i]
            rows.append(weights[b] * (values * values))
        field = jnp.concatenate(rows, axis=0)
        top, rest = halves(field)
        count = field.shape[0]
        dims = (((1,), (1,)), ((), ()))
        both = lax.dot_general(
            high[...], jnp.concatenate([top, rest], axis=0), dims, preferred_element_type=F32
        )
        small = lax.dot_general(low[...], top, dims, preferred_element_type=F32)
        out[pl.ds(i, planes, stride=extent), :] = both[:, :count] + both[:, count:] + small


def box_depth(eta_boxes, weights, tables):
    high, low = tables
    boxes, extent, span, depth = eta_boxes.shape
    planes = high.shape[0]
    return pl.pallas_call(
        depth_kernel,
        out_shape=jax.ShapeDtypeStruct((planes * extent, boxes * span), F32),
        in_specs=[
            pl.BlockSpec(memory_space=pltpu.SMEM),
            whole(eta_boxes),
            whole(high),
            whole(low),
        ],
        out_specs=pl.BlockSpec((planes * extent, boxes * span), lambda: (0, 0)),
        compiler_params=params(24),
        name="box_depth",
    )(weights, eta_boxes, high, low)


def rows_kernel(shape, place, boxes, high, low, out, lines, packed):
    owners, per_owner, half, extent, span, length, cols, over, slots, packs = shape
    step = pl.program_id(0)
    lane = lax.broadcasted_iota(jnp.int32, (extent, LANES), 1)
    side = lines.shape[0]

    @pl.when(step == 0)
    def _():
        packed[...] = jnp.zeros(packed.shape, F32)

    @pl.when((step == 0) | ((step >= 2) & (step <= half)))
    def _():
        lines[...] = jnp.zeros(lines.shape, F32)

        def add_owner(s, carry):
            for b in range(per_owner):
                at = s * per_owner + b
                first = pl.multiple_of(place[2 * at], STEP)
                column = place[2 * at + 1]
                inside = (lane >= b * span) & (lane < (b + 1) * span)
                shift = lax.rem(column + (LANES - b * span), LANES)
                for ri in range(2):
                    moved = pltpu.roll(jnp.where(inside, boxes[s, ri, 0], 0.0), shift, axis=1)
                    where_to = pl.ds(first, extent)
                    lines[0, ri, where_to, :] += jnp.where(lane >= column, moved, 0.0)
                    if side > 1:

                        @pl.when(column + span > LANES)
                        def _():
                            lines[1, ri, where_to, :] += jnp.where(lane < column, moved, 0.0)

            return carry

        lax.fori_loop(0, owners, add_owner, 0)
        lines[:, :, :extent, :] += lines[:, :, length:, :]

    sign = jnp.where(step == 1, -1.0, 1.0).astype(F32)

    for k in range(half + 1):
        slot = half if k == 1 else max(k - 1, 0)

        @pl.when(step == k)
        def _(slot=slot):
            lanes_all = lax.broadcasted_iota(jnp.int32, (length, LANES), 1)
            for ri in range(2):
                beyond = lines[side - 1, ri, :length, :]
                if side == 1:
                    beyond = jnp.where(lanes_all >= cols, beyond, 0.0)
                shift = ((slot % slots) * over - (cols % LANES)) % LANES
                if shift:
                    beyond = pltpu.roll(beyond, shift, axis=1)
                packed[slot // slots, ri] += beyond * (sign if ri else 1.0)

    for k in range(packs):

        @pl.when(step == half + 1 + k)
        def _(k=k):
            lines[0, :, :length, :] = packed[k]

    part = length // RADIX
    terms = []
    for l in range(RADIX):
        take = pl.ds(l, part, stride=RADIX)
        values = jnp.concatenate([lines[0, 0, take, :], lines[0, 1, take, :] * sign], axis=0)
        terms.append(table_first(high[l], low[l], values))
    real, imag = [v[:part] for v in terms], [v[part:] for v in terms]
    root = math.sqrt(0.75)
    sum_re, sum_im = real[1] + real[2], imag[1] + imag[2]
    dif_re, dif_im = root * (real[1] - real[2]), root * (imag[1] - imag[2])
    mid_re, mid_im = real[0] - 0.5 * sum_re, imag[0] - 0.5 * sum_im
    result_re = jnp.concatenate([real[0] + sum_re, mid_re + dif_im, mid_re - dif_im], axis=0)
    result_im = jnp.concatenate([imag[0] + sum_im, mid_im - dif_re, mid_im + dif_re], axis=0)
    block = (out.shape[0], out.shape[3], LANES)
    out[:, 0, 0] = result_re.reshape(block)[:, :, :cols]
    out[:, 1, 0] = result_im.reshape(block)[:, :, :cols]


def box_rows(pieces, place, tables, shape, parts):
    owners, per_owner, half, extent, span, length, cols, over, slots, packs = shape
    high, low = tables
    planes = half + 1 + packs
    rows = length // parts
    side = -(-(cols + over) // LANES)

    def plane_out(k, place):
        return (0, 0, jnp.where(k == 1, half, jnp.where(k > half, k, jnp.maximum(k - 1, 0))), 0, 0)

    return pl.pallas_call(
        functools.partial(rows_kernel, shape),
        out_shape=jax.ShapeDtypeStruct((parts, 2, planes, rows, cols), F32),
        grid_spec=pltpu.PrefetchScalarGridSpec(
            num_scalar_prefetch=1,
            grid=(planes,),
            in_specs=[
                pl.BlockSpec(
                    (owners, 2, 1, extent, LANES),
                    lambda k, place: (0, 0, jnp.clip(k - 1, 0, half - 1), 0, 0),
                ),
                whole(high),
                whole(low),
            ],
            out_specs=pl.BlockSpec((parts, 2, 1, rows, cols), plane_out),
            scratch_shapes=[
                pltpu.VMEM((side, 2, length + extent, LANES), F32),
                pltpu.VMEM((packs, 2, length, LANES), F32),
            ],
        ),
        compiler_params=params(44),
        name="box_rows",
    )(place, pieces, high, low)


def columns_kernel(slots, over, has_packs, main, conj, *rest):
    if has_packs:
        pack, conj_pack = rest[:2]
        rest = rest[2:]
    own, mirror, first_gain, conj_gain, fwd_high, fwd_low, inv_high, inv_low, out, scratch = rest
    step = pl.program_id(0)
    parts, rows, cols = out.shape[0], out.shape[3], out.shape[4]
    half_length = fwd_high.shape[1] // 2

    def gathered(body, overhang, slot):
        pieces = []
        for ri in range(2):
            line = []
            for q in range(parts):
                piece = body[q, ri, 0]
                if has_packs:
                    lane = lax.broadcasted_iota(jnp.int32, piece.shape, 1)
                    shift = lax.rem(cols - over * slot, cols)
                    beyond = pltpu.roll(overhang[(q - 1) % parts, ri, 0], shift, axis=1)
                    piece = piece + jnp.where(lane < over, beyond, 0.0)
                line.append(piece)
            pieces.append(jnp.concatenate(line, axis=1) if parts > 1 else line[0])
        lower = [v[:, :half_length] for v in pieces]
        upper = [v[:, half_length:] for v in pieces]
        even = jnp.concatenate([a + b for a, b in zip(lower, upper)], axis=1)
        odd = jnp.concatenate([a - b for a, b in zip(lower, upper)], axis=1)
        return even, odd

    def forward(body, overhang, slot):
        even, odd = gathered(body, overhang, slot)
        return (
            table_last(even, fwd_high[0], fwd_low[0]),
            table_last(odd, fwd_high[1], fwd_low[1]),
        )

    def scaled(spectrum, gain):
        even, odd = spectrum
        left, right = gain[:, :half_length], gain[:, half_length:]
        left = jnp.concatenate([left, left], axis=1)
        right = jnp.concatenate([right, right], axis=1)
        return even * left, odd * right

    gain = jnp.where(step == 0, first_gain[...], own[0] + mirror[0])
    slot = lax.rem(step, slots)
    even, odd = scaled(forward(main, pack if has_packs else None, slot), gain)
    scratch[0] = even
    scratch[1] = odd

    @pl.when(step == 0)
    def _():
        slot = pl.num_programs(0) % slots
        even, odd = scaled(forward(conj, conj_pack if has_packs else None, slot), conj_gain[...])
        scratch[0] += even
        scratch[1] += odd

    even = table_last(scratch[0], inv_high[0], inv_low[0])
    odd = table_last(scratch[1], inv_high[1], inv_low[1])
    lower, upper = even + odd, even - odd
    for ri in range(2):
        take = slice(ri * half_length, (ri + 1) * half_length)
        line = jnp.concatenate([lower[:, take], upper[:, take]], axis=1)
        for q in range(parts):
            out[q, ri, 0] = line[:, q * cols : (q + 1) * cols]


def grid_columns(arrived, own, mirror, first_gain, conj_gain, forward, inverse, slots, over, packs):
    parts, _, planes, rows, cols = arrived.shape
    half = own.shape[0]
    length = own.shape[2]
    has_packs = packs > 0
    one = (parts, 2, 1, rows, cols)
    operands = [arrived, arrived]
    specs = [
        pl.BlockSpec(one, lambda t: (0, 0, t, 0, 0)),
        pl.BlockSpec(one, lambda t: (0, 0, half, 0, 0)),
    ]
    if has_packs:
        operands += [arrived, arrived]
        specs += [
            pl.BlockSpec(one, lambda t: (0, 0, half + 1 + t // slots, 0, 0)),
            pl.BlockSpec(one, lambda t: (0, 0, half + 1 + half // slots, 0, 0)),
        ]
    gain_spec = pl.BlockSpec((1, rows, length), lambda t: (t, 0, 0))
    tables = [*forward, *inverse]
    return pl.pallas_call(
        functools.partial(columns_kernel, slots, over, has_packs),
        out_shape=jax.ShapeDtypeStruct((parts, 2, half, rows, cols), F32),
        grid=(half,),
        in_specs=specs
        + [gain_spec, gain_spec, whole(first_gain), whole(conj_gain)]
        + [whole(t) for t in tables],
        out_specs=pl.BlockSpec(one, lambda t: (0, 0, t, 0, 0)),
        scratch_shapes=[pltpu.VMEM((2, rows, length), F32)],
        compiler_params=params(44),
        name="grid_columns",
    )(*operands, own, mirror, first_gain, conj_gain, *tables)


def back_rows_kernel(body, high, low, out):
    parts, rows, cols = body.shape[0], body.shape[3], body.shape[4]
    length = parts * rows
    part = length // RADIX
    owners, group = out.shape[0], out.shape[3] // RADIX
    real = body[:, 0, 0].reshape(length, cols)
    imag = body[:, 1, 0].reshape(length, cols)
    real = [real[t * part : (t + 1) * part] for t in range(RADIX)]
    imag = [imag[t * part : (t + 1) * part] for t in range(RADIX)]
    root = math.sqrt(0.75)
    sum_re, sum_im = real[1] + real[2], imag[1] + imag[2]
    dif_re, dif_im = root * (real[1] - real[2]), root * (imag[1] - imag[2])
    mid_re, mid_im = real[0] - 0.5 * sum_re, imag[0] - 0.5 * sum_im
    terms = [
        (real[0] + sum_re, imag[0] + sum_im),
        (mid_re - dif_im, mid_im + dif_re),
        (mid_re + dif_im, mid_im - dif_re),
    ]
    for l in range(RADIX):
        result = table_first(high[l], low[l], jnp.concatenate(terms[l], axis=0))
        for ri in range(2):
            values = result[ri * part : (ri + 1) * part].reshape(owners, group, cols)
            out[:, ri, 0, l * group : (l + 1) * group, :] = values


def back_rows(arrived, tables, owners):
    high, low = tables
    parts, _, half, rows, cols = arrived.shape
    length = parts * rows
    return pl.pallas_call(
        back_rows_kernel,
        out_shape=jax.ShapeDtypeStruct((owners, 2, half, length // owners, cols), F32),
        grid=(half,),
        in_specs=[
            pl.BlockSpec((parts, 2, 1, rows, cols), lambda t: (0, 0, t, 0, 0)),
            whole(high),
            whole(low),
        ],
        out_specs=pl.BlockSpec((owners, 2, 1, length // owners, cols), lambda t: (0, 0, t, 0, 0)),
        compiler_params=params(44),
        name="back_rows",
    )(arrived, high, low)


def back_depth_kernel(rows, body, high, low, out):
    planes = high.shape[0]
    group = out.shape[0]
    dims = (((0,), (0,)), ((), ()))
    for g in range(group):
        for l in range(RADIX):
            values = body[pl.ds(l * group + g, planes, stride=rows), :]
            top, rest = halves(values)
            total = lax.dot_general(top, high[...], dims, preferred_element_type=F32)
            total += lax.dot_general(rest, high[...], dims, preferred_element_type=F32)
            total += lax.dot_general(top, low[...], dims, preferred_element_type=F32)
            out[g, l] = total


def back_depth(arrived, tables):
    high, low = tables
    planes, depth = high.shape
    rows, cols = arrived.shape[-2:]
    body = arrived.reshape(planes * rows, cols)
    group = rows // RADIX
    found = pl.pallas_call(
        functools.partial(back_depth_kernel, rows),
        out_shape=jax.ShapeDtypeStruct((group, RADIX, cols, depth), F32),
        in_specs=[whole(body), whole(high), whole(low)],
        out_specs=pl.BlockSpec((group, RADIX, cols, depth), lambda: (0, 0, 0, 0)),
        compiler_params=params(48),
        name="back_depth",
    )(body, high, low)
    return found.reshape(rows, cols, depth)


def mirror_kernel(index, own, other, edge, straight, mirrored, flip, own_out, mirror_out):
    rows, length = own.shape[1], own.shape[2]
    top, rest = halves(own[0])
    both = dot(jnp.concatenate([top, rest], axis=0), straight[...])
    own_out[0] = both[:rows] + both[rows:]
    top, rest = halves(other[0])
    turned = dot(flip[...], jnp.concatenate([top, rest], axis=1))
    edge_top, edge_rest = halves(edge[0])
    row = lax.broadcasted_iota(jnp.int32, (rows, length), 0)
    top = jnp.where(row == 0, edge_top.astype(F32), turned[:, :length])
    rest = jnp.where(row == 0, edge_rest.astype(F32), turned[:, length:])
    both = dot(jnp.concatenate([top, rest], axis=0).astype(BF16), mirrored[...])
    mirror_out[0] = both[:rows] + both[rows:]


def mirror_planes(green, edge, index, count, tables):
    rows, length = green.shape[1:]
    block = (1, rows, length)
    out = jax.ShapeDtypeStruct((count, rows, length), F32)
    return pl.pallas_call(
        mirror_kernel,
        out_shape=[out, out],
        grid_spec=pltpu.PrefetchScalarGridSpec(
            num_scalar_prefetch=1,
            grid=(count,),
            in_specs=[
                pl.BlockSpec(block, lambda t, index: (index[t], 0, 0)),
                pl.BlockSpec(block, lambda t, index: (index[count + t], 0, 0)),
                pl.BlockSpec((1, 1, length), lambda t, index: (index[count + t], 0, 0)),
            ]
            + [whole(t) for t in tables],
            out_specs=[pl.BlockSpec(block, lambda t, index: (t, 0, 0))] * 2,
        ),
        compiler_params=params(24),
        name="mirror_planes",
    )(index, green, green, edge, *tables)


def multiplier(green, px, py):
    own, rows, length = green.shape
    half = own // 2
    middle = px // 2
    p = lax.axis_index("px")
    tables = mirror_tables(rows, length)
    edge = from_behind(green[:, :1, :], "py", -1)
    zeros = jnp.zeros((2,), jnp.int32)
    own_zero, mirror_zero = mirror_planes(green, edge, zeros, 1, tables)
    mirror_zero = lax.ppermute(mirror_zero, "py", [(i, py - 1 - i) for i in range(py)])
    payload = jnp.where(p == 0, 0.5 * (own_zero + mirror_zero), mirror_zero)
    pairs = [(0, middle)] + [(i, px - i) for i in range(1, middle)]
    from_zero = lax.ppermute(payload, "px", pairs)
    lower = (p < middle).astype(jnp.int32)
    t = jnp.arange(half, dtype=jnp.int32)
    index = jnp.concatenate([t + lower, jnp.minimum(own - 1 - t + lower, own - 1)])
    own_planes, mirror = mirror_planes(green, edge, index, half, tables)
    pairs = [
        (a * py + b, (px - 1 - a) * py + py - 1 - b) for a in range(px) for b in range(py)
    ]
    mirror = lax.ppermute(mirror, ("px", "py"), pairs)
    middle_own = 0.5 * (own_zero + mirror_zero)
    first = own_planes[:1] + jnp.where(p < middle, mirror[:1], from_zero)
    first = jnp.where(p == middle, middle_own + from_zero, first)
    conj = jnp.where(p == middle, middle_own - from_zero, 0.0)
    return first[0], conj[0], own_planes, mirror


def exchange(shard, axis):
    return lax.all_to_all(shard, axis, split_axis=0, concat_axis=0, tiled=True)


def occupancy_window(squares, start_x, start_y, rows_dev, cols_dev, over_x, over_y):
    box_count, _, _, depth = squares.shape
    zero = jnp.zeros((), jnp.int32)
    patch = jnp.zeros((rows_dev + over_x, cols_dev + over_y, depth), F32)
    for b in range(box_count):
        position = (start_x[b], start_y[b], zero)
        current = lax.dynamic_slice(patch, position, squares.shape[1:])
        patch = lax.dynamic_update_slice(patch, current + squares[b], position)
    beside_x = from_behind(patch[rows_dev:], "px", 1)
    patch = patch[:rows_dev].at[:over_x].add(beside_x)
    beside_y = from_behind(patch[:, cols_dev:], "py", 1)
    return patch[:, :cols_dev].at[:, :over_y].add(beside_y)


def extended(field, over_x, over_y):
    px, py = lax.axis_size("px"), lax.axis_size("py")
    right = from_behind(field[:, :over_y], "py", -1)
    below = from_behind(field[:over_x], "px", -1)
    pairs = [
        (a * py + b, ((a - 1) % px) * py + (b - 1) % py) for a in range(px) for b in range(py)
    ]
    corner = lax.ppermute(field[:over_x, :over_y], ("px", "py"), pairs)
    upper = jnp.concatenate([field, right], axis=1)
    lower = jnp.concatenate([below, corner], axis=1)
    return jnp.concatenate([upper, lower], axis=0)


def on_device(eta_boxes, corners, grain_ids, misfit, green):
    px, py = lax.axis_size("px"), lax.axis_size("py")
    box_count, extent, span, depth = eta_boxes.shape
    own, kx_rows, length_y = green.shape
    length_x = kx_rows * py
    rows_dev = length_x // px
    cols_dev = length_y // py
    over_x = extent - STEP
    over_y = span - STEP
    half = own // 2
    slots = cols_dev // over_y
    packs = -(-(half + 1) // slots)
    first_x = corners[:, 0] * STEP
    start_x = first_x - lax.axis_index("px") * rows_dev
    start_y = corners[:, 1] * STEP - lax.axis_index("py") * cols_dev
    variant = jnp.arange(misfit.shape[0], dtype=jnp.int32)
    weights = jnp.sum(
        jnp.where(grain_ids[:, None] == variant[None, :], misfit[None, :], 0.0), axis=1
    )
    place = lax.all_gather(jnp.stack([first_x, start_y], axis=1), "px", tiled=True).reshape(-1)
    scale = 1.0 / (length_x * length_y * depth)
    depth_forward, depth_inverse = depth_tables(depth, px, scale)
    rows_forward, rows_inverse = row_tables(length_x)
    cols_forward, cols_inverse = column_tables(length_y)

    first_gain, conj_gain, own_planes, mirror = multiplier(green, px, py)

    spectra = box_depth(eta_boxes, weights, depth_forward)
    spectra = spectra.reshape(px, 2, half, extent, box_count * span)
    spectra = exchange(spectra, "px")
    shape = (px, box_count, half, extent, span, length_x, cols_dev, over_y, slots, packs)
    along_x = box_rows(spectra, place, rows_forward, shape, py)
    along_x = exchange(along_x, "py")
    if cols_dev % LANES:
        body = along_x[:, :, : half + 1]
        shifted = jnp.roll(along_x[:, :, half + 1 :], 1, axis=0)
        pieces = []
        for k in range(half + 1):
            at = (k % slots) * over_y
            pieces.append(shifted[:, :, k // slots, :, at : at + over_y])
        beyond = jnp.stack(pieces, axis=2)
        body = body.at[..., :over_y].add(beyond)
        body = jnp.transpose(body, (1, 2, 3, 0, 4)).reshape(1, 2, half + 1, kx_rows, length_y)
        back = grid_columns(
            body, own_planes, mirror, first_gain, conj_gain, cols_forward, cols_inverse, slots, over_y, 0
        )
        back = back.reshape(2, half, kx_rows, py, cols_dev)
        back = jnp.transpose(back, (3, 0, 1, 2, 4))
    else:
        back = grid_columns(
            along_x, own_planes, mirror, first_gain, conj_gain, cols_forward, cols_inverse, slots, over_y, packs
        )
    back = exchange(back, "py")
    back = back_rows(back, rows_inverse, px)
    back = exchange(back, "px")
    potential = back_depth(back, depth_inverse)

    occupancy = occupancy_window(
        eta_boxes * eta_boxes, start_x, start_y, rows_dev, cols_dev, over_x, over_y
    )
    occupancy = extended(occupancy, over_x, over_y)
    window = extended(potential, over_x, over_y)
    zero = jnp.zeros((), jnp.int32)
    results = []
    for b in range(box_count):
        position = (start_x[b], start_y[b], zero)
        mu = lax.dynamic_slice(window, position, eta_boxes.shape[1:])
        total = lax.dynamic_slice(occupancy, position, eta_boxes.shape[1:])
        results.append(advance(eta_boxes[b], weights[b], mu, total))
    return (jnp.stack(results), potential)


def solution(mesh):
    in_specs = (
        P(("px", "py"), None, None, None),
        P(("px", "py"), None),
        P(("px", "py")),
        P(),
        P("px", "py", None),
    )
    out_specs = (P(("px", "py"), None, None, None), P("px", "py", None))
    return jax.shard_map(
        on_device, mesh=mesh, in_specs=in_specs, out_specs=out_specs, check_vma=False
    )
```

```python
import functools
import math

import jax
import jax.numpy as jnp
import ml_dtypes
import numpy as np
from jax import lax
from jax.experimental import pallas as pl
from jax.experimental.pallas import tpu as pltpu
from jax.sharding import PartitionSpec as P

STEP = 8
LANES = 128
RADIX = 3

rate_step = 0.2
gradient_coef = 0.1
coupling = 1.5

F32 = jnp.float32
BF16 = jnp.bfloat16
MIB = 1 << 20


def from_behind(shard, axis, by):
    peers = lax.axis_size(axis)
    return lax.ppermute(shard, axis, [(i, (i + by) % peers) for i in range(peers)])


def laplace(values):
    padded = jnp.pad(values, ((1, 1), (1, 1), (0, 0)))
    beside_all = padded[2:, 1:-1] + padded[:-2, 1:-1] + padded[1:-1, 2:] + padded[1:-1, :-2]
    beside_all = beside_all + jnp.roll(values, 1, axis=2) + jnp.roll(values, -1, axis=2)
    return beside_all - 6.0 * values


def advance(order_param, occupancy):
    square = order_param * order_param
    force = order_param * square - order_param + 2.0 * coupling * order_param * (occupancy - square)
    force = force - gradient_coef * laplace(order_param)
    return order_param - rate_step * force


def pair_of(table):
    high = table.astype(ml_dtypes.bfloat16)
    low = (table - high.astype(np.float64)).astype(ml_dtypes.bfloat16)
    return high, low


def angle_of(index, length):
    return (index % length) * (2.0 * math.pi / length)


def depth_tables(depth, owners, chunks, scale):
    own = depth // owners
    half = own // 2
    z = np.arange(depth)

    def rows_of(p, planes):
        forward, inverse = ([], []), ([], [])
        for t in planes:
            angles = angle_of((own * p + t + (1 if p < owners // 2 else 0)) * z, depth)
            c, s, factor = np.cos(angles), np.sin(angles), scale
            if p == owners // 2 and t == 0:
                s, factor = -np.ones(depth), 0.5 * scale
            forward[0].append(c)
            forward[1].append(-s)
            inverse[0].append(factor * c)
            inverse[1].append(-factor * s)
        return forward[0] + forward[1], inverse[0] + inverse[1]

    out = []
    for p in range(owners):
        out += rows_of(p, range(half))[0]
    back = []
    size = half // chunks
    for k in range(chunks):
        for p in range(owners):
            back += rows_of(p, range(k * size, (k + 1) * size))[1]
    return pair_of(np.array(out)), pair_of(np.array(back))


def row_tables(length):
    part = length // RADIX
    m = np.arange(part)
    forward, inverse = [], []
    for l in range(RADIX):
        angles = angle_of(m[:, None] * (RADIX * m[None, :] + l), length)
        c, s = np.cos(angles), np.sin(angles)
        forward.append(np.block([[c, s], [-s, c]]))
        c, s = c.T, s.T
        inverse.append(np.block([[c, -s], [s, c]]))
    return pair_of(np.array(forward)), pair_of(np.array(inverse))


def column_tables(length):
    part = length // 2
    m = np.arange(part)
    forward, inverse = [], []
    for parity in range(2):
        angles = angle_of(m[:, None] * (2 * m[None, :] + parity), length)
        c, s = np.cos(angles), np.sin(angles)
        forward.append(np.block([[c, -s], [s, c]]))
        c, s = c.T, s.T
        inverse.append(np.block([[c, s], [-s, c]]))
    return pair_of(np.array(forward)), pair_of(np.array(inverse))


def mirror_tables(rows, length):
    part = length // 2
    m = np.arange(part)
    order = np.concatenate([2 * m, 2 * m + 1])
    straight = np.zeros((length, length))
    straight[order, np.arange(length)] = 1.0
    mirrored = np.zeros((length, length))
    mirrored[(length - order) % length, np.arange(length)] = 1.0
    flip = np.zeros((rows, rows))
    i = np.arange(1, rows)
    flip[i, rows - i] = 1.0
    as_bf16 = lambda table: table.astype(ml_dtypes.bfloat16)
    return as_bf16(straight), as_bf16(mirrored), as_bf16(flip)


def halves(values):
    high = values.astype(BF16)
    return high, (values - high.astype(F32)).astype(BF16)


def dot(a, b):
    return jnp.dot(a, b, preferred_element_type=F32)


def table_first(high, low, values):
    top, rest = halves(values)
    width = values.shape[1]
    if width % LANES == 0:
        both = dot(high, jnp.concatenate([top, rest], axis=1))
        both = both[:, :width] + both[:, width:]
    else:
        both = dot(high, top) + dot(high, rest)
    return both + dot(low, top)


def table_last(values, high, low):
    top, rest = halves(values)
    rows = values.shape[0]
    both = dot(jnp.concatenate([top, rest], axis=0), high)
    return both[:rows] + both[rows:] + dot(top, low)


def cost(*arrays):
    size = sum(math.prod(array.shape) * 4 for array in arrays)
    return pl.CostEstimate(flops=0, bytes_accessed=5 * size, transcendentals=0)


def params(mib):
    return pltpu.CompilerParams(vmem_limit_bytes=mib * MIB)


ANYWHERE = pl.BlockSpec(memory_space=pl.ANY)


def waiting(kernel, before, after):
    def body(*refs):
        kernel(*refs[:before], *refs[before + len(after) :])

    return body


def whole(array):
    rank = len(array.shape)
    return pl.BlockSpec(array.shape, lambda *_: (0,) * rank)


def depth_kernel(weights, place, eta, high, low, out):
    boxes, extent, span = eta.shape[0], eta.shape[1], eta.shape[2]
    owners = out.shape[0]
    planes = high.shape[0] // owners
    dims = (((1,), (1,)), ((), ()))
    for i in range(extent):
        rows = []
        for b in range(boxes):
            values = eta[b, i]
            rows.append(weights[b] * (values * values))
        field = jnp.concatenate(rows, axis=0)
        top, rest = halves(field)
        count = field.shape[0]
        both = lax.dot_general(
            high[...], jnp.concatenate([top, rest], axis=0), dims, preferred_element_type=F32
        )
        small = lax.dot_general(low[...], top, dims, preferred_element_type=F32)
        result = both[:, :count] + both[:, count:] + small
        for p in range(owners):
            out[p, pl.ds(i, planes, stride=extent), :] = result[p * planes : (p + 1) * planes]
    lane = lax.broadcasted_iota(jnp.int32, (STEP, boxes * span), 1)
    where_to = jnp.zeros(lane.shape, jnp.int32)
    for k in range(2 * boxes):
        where_to = jnp.where(lane == k, place[k], where_to)
    for p in range(owners):
        out[p, planes * extent :, :] = where_to.astype(F32)


def box_depth(eta_boxes, weights, place, tables, owners, after):
    high, low = tables
    boxes, extent, span, depth = eta_boxes.shape
    shape = (owners, high.shape[0] // owners * extent + STEP, boxes * span)
    return pl.pallas_call(
        waiting(depth_kernel, 5, after),
        out_shape=jax.ShapeDtypeStruct(shape, F32),
        in_specs=[
            pl.BlockSpec(memory_space=pltpu.SMEM),
            pl.BlockSpec(memory_space=pltpu.SMEM),
            whole(eta_boxes),
            whole(high),
            whole(low),
            *([ANYWHERE] * len(after)),
        ],
        out_specs=pl.BlockSpec(shape, lambda: (0, 0, 0)),
        compiler_params=params(24),
        cost_estimate=cost(eta_boxes, eta_boxes),
        name="box_depth",
    )(weights, place, eta_boxes, high, low, *after)


def rows_kernel(shape, place, boxes_re, boxes_im, high, low, out, lines, packed):
    owners, per_owner, half, extent, span, length, cols, over, slots, packs = shape
    step = pl.program_id(0)
    lane = lax.broadcasted_iota(jnp.int32, (extent, LANES), 1)
    side = lines.shape[0]

    @pl.when(step == 0)
    def _():
        packed[...] = jnp.zeros(packed.shape, F32)

    @pl.when((step <= half) & (step != 1))
    def _():
        lines[...] = jnp.zeros(lines.shape, F32)

        def add_owner(s, carry):
            values = (boxes_re[s], boxes_im[s])
            moved = []
            for b in range(per_owner):
                column = place[2 * (s * per_owner + b) + 1]
                inside = (lane >= b * span) & (lane < (b + 1) * span)
                shift = lax.rem(column + (LANES - b * span), LANES)
                for v in values:
                    moved.append(pltpu.roll(jnp.where(inside, v, 0.0), shift, axis=1))
            for b in range(per_owner):
                at = 2 * (s * per_owner + b)
                where_to = pl.ds(pl.multiple_of(place[at], STEP), extent)
                here = lane >= place[at + 1]
                for ri in range(2):
                    value = moved[2 * b + ri]
                    lines[0, ri, where_to, :] += jnp.where(here, value, 0.0)
                    if side > 1:
                        lines[1, ri, where_to, :] += jnp.where(here, 0.0, value)
            return carry

        lax.fori_loop(0, owners, add_owner, 0, unroll=4)
        lines[:, :, :extent, :] += lines[:, :, length:, :]

    sign = jnp.where(step == 1, -1.0, 1.0).astype(F32)

    for k in range(half + 1):
        slot = half if k == 1 else max(k - 1, 0)

        @pl.when(step == k)
        def _(slot=slot):
            lanes_all = lax.broadcasted_iota(jnp.int32, (length, LANES), 1)
            for ri in range(2):
                beyond = lines[side - 1, ri, :length, :]
                if side == 1:
                    beyond = jnp.where(lanes_all >= cols, beyond, 0.0)
                shift = ((slot % slots) * over - (cols % LANES)) % LANES
                if shift:
                    beyond = pltpu.roll(beyond, shift, axis=1)
                packed[slot // slots, ri] += beyond * (sign if ri else 1.0)

    for k in range(packs):

        @pl.when(step == half + 1 + k)
        def _(k=k):
            lines[0, :, :length, :] = packed[k]

    part = length // RADIX
    terms = []
    for l in range(RADIX):
        take = pl.ds(l, part, stride=RADIX)
        values = jnp.concatenate([lines[0, 0, take, :], lines[0, 1, take, :] * sign], axis=0)
        terms.append(table_first(high[l], low[l], values))
    real, imag = [v[:part] for v in terms], [v[part:] for v in terms]
    root = math.sqrt(0.75)
    sum_re, sum_im = real[1] + real[2], imag[1] + imag[2]
    dif_re, dif_im = root * (real[1] - real[2]), root * (imag[1] - imag[2])
    mid_re, mid_im = real[0] - 0.5 * sum_re, imag[0] - 0.5 * sum_im
    result_re = jnp.concatenate([real[0] + sum_re, mid_re + dif_im, mid_re - dif_im], axis=0)
    result_im = jnp.concatenate([imag[0] + sum_im, mid_im - dif_re, mid_im + dif_re], axis=0)
    block = (out.shape[0], out.shape[3], LANES)
    out[:, 0, 0] = result_re.reshape(block)[:, :, :cols]
    out[:, 1, 0] = result_im.reshape(block)[:, :, :cols]


def box_rows(pieces, place, tables, shape, parts, after):
    owners, per_owner, half, extent, span, length, cols, over, slots, packs = shape
    high, low = tables
    planes = half + 1 + packs
    rows = length // parts
    side = -(-(cols + over) // LANES)

    def plane_in(k):
        return jnp.clip(k - 1, 0, half - 1)

    def plane_out(k, place):
        return (0, 0, jnp.where(k == 1, half, jnp.where(k > half, k, jnp.maximum(k - 1, 0))), 0, 0)

    return pl.pallas_call(
        waiting(functools.partial(rows_kernel, shape), 5, after),
        out_shape=jax.ShapeDtypeStruct((parts, 2, planes, rows, cols), F32),
        grid_spec=pltpu.PrefetchScalarGridSpec(
            num_scalar_prefetch=1,
            grid=(planes,),
            in_specs=[
                pl.BlockSpec((owners, extent, LANES), lambda k, place: (0, plane_in(k), 0)),
                pl.BlockSpec((owners, extent, LANES), lambda k, place: (0, half + plane_in(k), 0)),
                whole(high),
                whole(low),
                *([ANYWHERE] * len(after)),
            ],
            out_specs=pl.BlockSpec((parts, 2, 1, rows, cols), plane_out),
            scratch_shapes=[
                pltpu.VMEM((side, 2, length + extent, LANES), F32),
                pltpu.VMEM((packs, 2, length, LANES), F32),
            ],
        ),
        compiler_params=params(56),
        cost_estimate=cost(pieces, jax.ShapeDtypeStruct((parts, 2, planes, rows, cols), F32)),
        name="box_rows",
    )(place, pieces, pieces, high, low, *after)


def columns_kernel(slots, over, has_packs, has_conj, begin, half, *refs):
    refs = list(refs)
    me = refs.pop(0)[0]
    main = refs.pop(0)
    pack = refs.pop(0) if has_packs else None
    conj = refs.pop(0) if has_conj else None
    conj_pack = refs.pop(0) if has_conj and has_packs else None
    own, mirror = refs.pop(0), refs.pop(0)
    first_gain, conj_gain = (refs.pop(0), refs.pop(0)) if has_conj else (None, None)
    fwd_high, fwd_low, inv_high, inv_low = refs[:4]
    out, scratch = refs[-2:]
    step = pl.program_id(0)
    parts, rows, cols = out.shape[0], out.shape[3], out.shape[4]
    half_length = fwd_high.shape[1] // 2

    def gathered(body, overhang, slot):
        pieces = []
        for ri in range(2):
            line = []
            for q in range(parts):
                piece = body[q, ri, 0]
                if has_packs:
                    lane = lax.broadcasted_iota(jnp.int32, piece.shape, 1)
                    shift = lax.rem(cols - over * slot, cols)
                    beyond = pltpu.roll(overhang[(q - 1) % parts, ri, 0], shift, axis=1)
                    piece = piece + jnp.where(lane < over, beyond, 0.0)
                line.append(piece)
            pieces.append(jnp.concatenate(line, axis=1) if parts > 1 else line[0])
        lower = [v[:, :half_length] for v in pieces]
        upper = [v[:, half_length:] for v in pieces]
        even = jnp.concatenate([a + b for a, b in zip(lower, upper)], axis=1)
        odd = jnp.concatenate([a - b for a, b in zip(lower, upper)], axis=1)
        return even, odd

    def forward(body, overhang, slot):
        even, odd = gathered(body, overhang, slot)
        return (
            table_last(even, fwd_high[0], fwd_low[0]),
            table_last(odd, fwd_high[1], fwd_low[1]),
        )

    def scaled(spectrum, gain):
        even, odd = spectrum
        left, right = gain[:, :half_length], gain[:, half_length:]
        left = jnp.concatenate([left, left], axis=1)
        right = jnp.concatenate([right, right], axis=1)
        return even * left, odd * right

    gain = own[0] + mirror[0]
    if has_conj:
        gain = jnp.where(step == 0, first_gain[...], gain)
    even, odd = scaled(forward(main, pack, lax.rem(step + begin, slots)), gain)
    scratch[0] = even
    scratch[1] = odd

    if has_conj:

        @pl.when(step == 0)
        def _():
            even, odd = scaled(forward(conj, conj_pack, half % slots), conj_gain[...])
            scratch[0] += even
            scratch[1] += odd

    even = table_last(scratch[0], inv_high[0], inv_low[0])
    odd = table_last(scratch[1], inv_high[1], inv_low[1])
    lower, upper = even + odd, even - odd
    for ri in range(2):
        take = slice(ri * half_length, (ri + 1) * half_length)
        line = jnp.concatenate([lower[:, take], upper[:, take]], axis=1)
        for q in range(parts):
            out[lax.rem(q - me + parts, parts), ri, 0] = line[:, q * cols : (q + 1) * cols]


def grid_columns(me, arrived, count, half, own, begin, mirror, gains, forward, inverse, slots, over, packs, after):
    parts, _, planes, rows, cols = arrived.shape
    length = own.shape[2]
    has_packs, has_conj = packs > 0, gains is not None
    one = (parts, 2, 1, rows, cols)
    operands = [me, arrived]
    specs = [
        pl.BlockSpec(memory_space=pltpu.SMEM),
        pl.BlockSpec(one, lambda t: (0, 0, begin + t, 0, 0)),
    ]
    if has_packs:
        operands += [arrived]
        specs += [pl.BlockSpec(one, lambda t: (0, 0, half + 1 + (begin + t) // slots, 0, 0))]
    if has_conj:
        operands += [arrived]
        specs += [pl.BlockSpec(one, lambda t: (0, 0, half, 0, 0))]
        if has_packs:
            operands += [arrived]
            specs += [pl.BlockSpec(one, lambda t: (0, 0, half + 1 + half // slots, 0, 0))]
    operands += [own, mirror]
    specs += [
        pl.BlockSpec((1, rows, length), lambda t: (begin + t, 0, 0)),
        pl.BlockSpec((1, rows, length), lambda t: (t, 0, 0)),
    ]
    fixed = [*(gains or ()), *forward, *inverse]
    return pl.pallas_call(
        functools.partial(columns_kernel, slots, over, has_packs, has_conj, begin, half),
        out_shape=jax.ShapeDtypeStruct((parts, 2, count, rows, cols), F32),
        grid=(count,),
        in_specs=specs + [whole(t) for t in fixed] + [ANYWHERE] * len(after),
        out_specs=pl.BlockSpec(one, lambda t: (0, 0, t, 0, 0)),
        scratch_shapes=[pltpu.VMEM((2, rows, length), F32)],
        compiler_params=params(56),
        cost_estimate=cost(jax.ShapeDtypeStruct((parts, 6, count, rows, cols), F32)),
        name="grid_columns",
    )(*operands, *fixed, *after)


def back_rows_kernel(count, *refs):
    me = refs[0][0]
    bodies = refs[1 : 1 + count]
    high, low, out, lines = refs[1 + count :]
    parts, rows, cols = lines.shape[0], lines.shape[2], lines.shape[3]
    length = parts * rows
    part = length // RADIX
    owners, group = out.shape[0], out.shape[3] // RADIX
    if count == 1:
        lines[...] = bodies[0][:, :, 0]
    else:
        for r, body in enumerate(bodies):
            lines[lax.rem(me - r + parts, parts)] = body[:, 0]
    real = lines[:, 0].reshape(length, cols)
    imag = lines[:, 1].reshape(length, cols)
    real = [real[t * part : (t + 1) * part] for t in range(RADIX)]
    imag = [imag[t * part : (t + 1) * part] for t in range(RADIX)]
    root = math.sqrt(0.75)
    sum_re, sum_im = real[1] + real[2], imag[1] + imag[2]
    dif_re, dif_im = root * (real[1] - real[2]), root * (imag[1] - imag[2])
    mid_re, mid_im = real[0] - 0.5 * sum_re, imag[0] - 0.5 * sum_im
    terms = [
        (real[0] + sum_re, imag[0] + sum_im),
        (mid_re - dif_im, mid_im + dif_re),
        (mid_re + dif_im, mid_im - dif_re),
    ]
    for l in range(RADIX):
        result = table_first(high[l], low[l], jnp.concatenate(terms[l], axis=0))
        for ri in range(2):
            values = result[ri * part : (ri + 1) * part].reshape(owners, group, cols)
            out[:, ri, 0, l * group : (l + 1) * group, :] = values


def back_rows(me, bodies, tables, owners, after):
    high, low = tables
    half, rows, cols = bodies[0].shape[-3:]
    if len(bodies) == 1:
        parts = bodies[0].shape[0]
        spec = pl.BlockSpec((parts, 2, 1, rows, cols), lambda t: (0, 0, t, 0, 0))
    else:
        parts = len(bodies)
        spec = pl.BlockSpec((2, 1, rows, cols), lambda t: (0, t, 0, 0))
    length = parts * rows
    out = jax.ShapeDtypeStruct((owners, 2, half, length // owners, cols), F32)
    return pl.pallas_call(
        waiting(functools.partial(back_rows_kernel, len(bodies)), len(bodies) + 3, after),
        out_shape=out,
        grid=(half,),
        in_specs=[pl.BlockSpec(memory_space=pltpu.SMEM)]
        + [spec] * len(bodies)
        + [whole(high), whole(low)]
        + [ANYWHERE] * len(after),
        out_specs=pl.BlockSpec((owners, 2, 1, length // owners, cols), lambda t: (0, 0, t, 0, 0)),
        scratch_shapes=[pltpu.VMEM((parts, 2, rows, cols), F32)],
        compiler_params=params(56),
        cost_estimate=cost(out, out),
        name="back_rows",
    )(me, *bodies, high, low, *after)


def back_depth_kernel(chunks, *refs):
    bodies = refs[:chunks]
    high, low = refs[chunks : chunks + 2]
    out = refs[-1]
    group = out.shape[0]
    planes = bodies[0].shape[0]
    dims = (((0,), (0,)), ((), ()))
    for g in range(group):
        for l in range(RADIX):
            lines = [body[:, l, g, :] for body in bodies]
            values = jnp.concatenate(lines, axis=0) if chunks > 1 else lines[0]
            top, rest = halves(values)
            total = lax.dot_general(top, high[...], dims, preferred_element_type=F32)
            total += lax.dot_general(rest, high[...], dims, preferred_element_type=F32)
            total += lax.dot_general(top, low[...], dims, preferred_element_type=F32)
            out[g, l] = total


def back_depth(arrived, tables, after, only=None):
    high, low = tables
    chunks = len(arrived)
    depth = high.shape[1]
    planes = high.shape[0] // chunks
    rows, cols = arrived[0].shape[-2:]
    group = rows // RADIX
    take = group if only is None else only // RADIX
    bodies = [piece.reshape(planes, RADIX, group, cols) for piece in arrived]
    block = (planes, RADIX, STEP, cols)
    found = pl.pallas_call(
        functools.partial(back_depth_kernel, chunks),
        out_shape=jax.ShapeDtypeStruct((take, RADIX, cols, depth), F32),
        grid=(take // STEP,),
        in_specs=[pl.BlockSpec(block, lambda g: (0, 0, g, 0)) for _ in bodies]
        + [whole(high), whole(low)]
        + [ANYWHERE] * len(after),
        out_specs=pl.BlockSpec((STEP, RADIX, cols, depth), lambda g: (g, 0, 0, 0)),
        compiler_params=params(56),
        cost_estimate=cost(*bodies, *bodies),
        name="back_depth",
    )(*bodies, high, low, *after)
    return found.reshape(take * RADIX, cols, depth)


def mirror_kernel(index, other, edge, mirrored, flip, out):
    rows, length = other.shape[1], other.shape[2]
    top, rest = halves(other[0])
    turned = dot(flip[...], jnp.concatenate([top, rest], axis=1))
    edge_top, edge_rest = halves(edge[0])
    row = lax.broadcasted_iota(jnp.int32, (rows, length), 0)
    top = jnp.where(row == 0, edge_top.astype(F32), turned[:, :length])
    rest = jnp.where(row == 0, edge_rest.astype(F32), turned[:, length:])
    both = dot(jnp.concatenate([top, rest], axis=0).astype(BF16), mirrored[...])
    out[0] = both[:rows] + both[rows:]


def mirror_planes(green, edge, index, mirrored, flip, after):
    rows, length = green.shape[1:]
    block = (1, rows, length)
    count = index.shape[0]
    return pl.pallas_call(
        waiting(mirror_kernel, 5, after),
        out_shape=jax.ShapeDtypeStruct((count, rows, length), F32),
        grid_spec=pltpu.PrefetchScalarGridSpec(
            num_scalar_prefetch=1,
            grid=(count,),
            in_specs=[
                pl.BlockSpec(block, lambda t, index: (index[t], 0, 0)),
                pl.BlockSpec((1, 1, length), lambda t, index: (index[t], 0, 0)),
                whole(mirrored),
                whole(flip),
                *([ANYWHERE] * len(after)),
            ],
            out_specs=pl.BlockSpec(block, lambda t, index: (t, 0, 0)),
        ),
        compiler_params=params(16),
        cost_estimate=cost(jax.ShapeDtypeStruct((count, rows, length), F32)),
        name="mirror_planes",
    )(index, green, edge, mirrored, flip, *after)


def order_kernel(index, own, straight, out):
    rows = own.shape[1]
    top, rest = halves(own[0])
    both = dot(jnp.concatenate([top, rest], axis=0), straight[...])
    out[0] = both[:rows] + both[rows:]


def order_planes(green, index, straight, after):
    rows, length = green.shape[1:]
    block = (1, rows, length)
    count = index.shape[0]
    return pl.pallas_call(
        waiting(order_kernel, 3, after),
        out_shape=jax.ShapeDtypeStruct((count, rows, length), F32),
        grid_spec=pltpu.PrefetchScalarGridSpec(
            num_scalar_prefetch=1,
            grid=(count,),
            in_specs=[
                pl.BlockSpec(block, lambda t, index: (index[t], 0, 0)),
                whole(straight),
                *([ANYWHERE] * len(after)),
            ],
            out_specs=pl.BlockSpec(block, lambda t, index: (t, 0, 0)),
        ),
        compiler_params=params(16),
        cost_estimate=cost(jax.ShapeDtypeStruct((count, rows, length), F32)),
        name="order_planes",
    )(index, green, straight, *after)


def edges_of(body, axis, first, last):
    over = first.shape[axis]
    if axis == 0:
        first[...] = body[:over]
        last[...] = body[body.shape[0] - over :]
    else:
        first[...] = body[:, :over, :]
        last[...] = body[:, body.shape[1] - over :, :]


def patch_kernel(place, eta, out, first, last):
    boxes, extent, span = eta.shape[0], eta.shape[1], eta.shape[2]
    out[...] = jnp.zeros(out.shape, F32)
    for b in range(boxes):
        row = place[2 * b]
        columns = pl.ds(pl.multiple_of(place[2 * b + 1], STEP), span)

        def add_row(i, carry, b=b, row=row, columns=columns):
            values = eta[b, i]
            out[row + i, columns, :] += values * values
            return carry

        lax.fori_loop(0, extent, add_row, 0, unroll=4)
    edges_of(out, 0, first, last)


def occupancy_patch(eta_boxes, place, rows, cols, over, after):
    depth = eta_boxes.shape[3]
    shapes = [(rows, cols, depth), (over, cols, depth), (over, cols, depth)]
    return pl.pallas_call(
        waiting(patch_kernel, 2, after),
        out_shape=[jax.ShapeDtypeStruct(shape, F32) for shape in shapes],
        in_specs=[pl.BlockSpec(memory_space=pltpu.SMEM), whole(eta_boxes)]
        + [ANYWHERE] * len(after),
        out_specs=[pl.BlockSpec(shape, lambda: (0, 0, 0)) for shape in shapes],
        compiler_params=params(32),
        cost_estimate=cost(eta_boxes),
        name="occupancy_patch",
    )(place, eta_boxes, *after)


def join_rows_kernel(body, behind, ahead, out, first, last):
    step, steps = pl.program_id(0), pl.num_programs(0)
    near = behind.shape[0] // out.shape[0]
    out[...] = body[...]
    count = out.shape[0]

    @pl.when(step < near)
    def _():
        out[...] += behind[pl.ds(step * count, count)]

    @pl.when(step >= steps - near)
    def _():
        out[...] += ahead[pl.ds((step - steps + near) * count, count)]

    edges_of(out, 1, first, last)


def join_rows(patch, behind, ahead, over, after):
    rows, cols, depth = patch.shape
    spec = pl.BlockSpec((STEP, cols, depth), lambda r: (r, 0, 0))
    side = pl.BlockSpec((STEP, over, depth), lambda r: (r, 0, 0))
    edge = jax.ShapeDtypeStruct((rows, over, depth), F32)
    return pl.pallas_call(
        waiting(join_rows_kernel, 3, after),
        out_shape=[jax.ShapeDtypeStruct(patch.shape, F32), edge, edge],
        grid=(rows // STEP,),
        in_specs=[spec, whole(behind), whole(ahead)] + [ANYWHERE] * len(after),
        out_specs=[spec, side, side],
        compiler_params=params(24),
        cost_estimate=cost(patch),
        name="join_rows",
    )(patch, behind, ahead, *after)


def apply_kernel(place, weights, base, eta, main, right, below, corner, out):
    boxes, extent, span = eta.shape[0], eta.shape[1], eta.shape[2]
    rows, cols = main.shape[0], main.shape[1]

    def one_box(b, carry):
        first, column = place[2 * b], place[2 * b + 1]
        factor = (-2.0 * rate_step) * weights[b]
        for i in range(0, extent, STEP):
            x = first + i
            for j in range(0, span, STEP):
                y = pl.multiple_of(column + j, STEP)
                for source, take in (
                    (main, (x < rows) & (y < cols)),
                    (right, (x < rows) & (y >= cols)),
                    (below, (x >= rows) & (y < cols)),
                    (corner, (x >= rows) & (y >= cols)),
                ):

                    @pl.when(take)
                    def _(source=source, i=i, j=j, x=x, y=y):
                        low = source is below or source is corner
                        side = source is right or source is corner
                        at_x = x - rows if low else x
                        at_y = pl.multiple_of(y - cols if side else y, STEP)
                        mu = source[pl.ds(at_x, STEP), pl.ds(at_y, STEP), :]
                        here = (b, pl.ds(i, STEP), pl.ds(j, STEP), slice(None))
                        out[here] = base[here] + factor * eta[here] * mu

        return carry

    lax.fori_loop(0, boxes, one_box, 0)


def apply_potential(place, weights, base, eta_boxes, pieces):
    arrays = [base, eta_boxes, *pieces]
    smem = pl.BlockSpec(memory_space=pltpu.SMEM)
    return pl.pallas_call(
        apply_kernel,
        out_shape=jax.ShapeDtypeStruct(eta_boxes.shape, F32),
        in_specs=[smem, smem] + [whole(v) for v in arrays],
        out_specs=whole(eta_boxes),
        compiler_params=params(36),
        cost_estimate=cost(eta_boxes, eta_boxes),
        name="apply_potential",
    )(place, weights, *arrays)


def exchange(shard, axis):
    return lax.all_to_all(shard, axis, split_axis=0, concat_axis=0, tiled=True)


def send_round(lines, axis):
    count = lines.shape[0]
    return [lines[0]] + [from_behind(lines[r], axis, r) for r in range(1, count)]


def potential_pieces(field, rows, over_x, over_y):
    px, py = lax.axis_size("px"), lax.axis_size("py")
    below = from_behind(rows, "px", -1)
    right = from_behind(field[:, :over_y], "py", -1)
    pairs = [
        (a * py + b, ((a - 1) % px) * py + (b - 1) % py) for a in range(px) for b in range(py)
    ]
    corner = lax.ppermute(rows[:, :over_y], ("px", "py"), pairs)
    return field, right, below, corner


def without_packs(along_x, count, slots, over, parts):
    body = count
    shifted = jnp.roll(along_x[:, :, body:], 1, axis=0)
    pieces = []
    for k in range(body):
        at = (k % slots) * over
        pieces.append(shifted[:, :, k // slots, :, at : at + over])
    body = along_x[:, :, :body].at[..., :over].add(jnp.stack(pieces, axis=2))
    body = jnp.transpose(body, (1, 2, 3, 0, 4))
    return body.reshape((1,) + body.shape[:3] + (-1,))


def on_device(eta_boxes, corners, grain_ids, misfit, green):
    px, py = lax.axis_size("px"), lax.axis_size("py")
    p = lax.axis_index("px")
    middle = px // 2
    box_count, extent, span, depth = eta_boxes.shape
    own, kx_rows, length_y = green.shape
    length_x = kx_rows * py
    rows_dev, cols_dev = length_x // px, length_y // py
    over_x, over_y = extent - STEP, span - STEP
    half = own // 2
    chunks = 2 if half % 2 == 0 else 1
    size = half // chunks
    slots = cols_dev // over_y
    first_x = corners[:, 0] * STEP
    start_x = first_x - p * rows_dev
    start_y = corners[:, 1] * STEP - lax.axis_index("py") * cols_dev
    place_here = jnp.stack([start_x, start_y], axis=1).reshape(-1)
    variant = jnp.arange(misfit.shape[0], dtype=jnp.int32)
    weights = jnp.sum(
        jnp.where(grain_ids[:, None] == variant[None, :], misfit[None, :], 0.0), axis=1
    )
    scale = 1.0 / (length_x * length_y * depth)
    depth_forward, depth_inverse = depth_tables(depth, px, chunks, scale)
    rows_forward, rows_inverse = row_tables(length_x)
    cols_forward, cols_inverse = column_tables(length_y)
    straight, mirrored, flip = mirror_tables(kx_rows, length_y)

    edge = from_behind(green[:, :1, :], "py", -1)
    place_send = jnp.stack([first_x, start_y], axis=1).reshape(-1)
    spectra = box_depth(eta_boxes, weights, place_send, depth_forward, px, ())
    arrived = exchange(spectra, "px")
    place = arrived[:, -STEP, : 2 * box_count].astype(jnp.int32).reshape(-1)

    lower = (p < middle).astype(jnp.int32)
    t = jnp.arange(half, dtype=jnp.int32)
    facing = [(i, py - 1 - i) for i in range(py)]
    zero_index = jnp.zeros((1,), jnp.int32)
    index = jnp.minimum(own - 1 - t + lower, own - 1)
    indices = [index[k * size : (k + 1) * size] for k in range(chunks)]
    indices.insert(1, zero_index)
    mirror = [spectra]
    for which in indices:
        mirror.append(mirror_planes(green, edge, which, mirrored, flip, (mirror[-1],)))
    own_index = jnp.concatenate([t + lower, zero_index])
    own_planes = order_planes(green, own_index, straight, (mirror[-1],))
    patch, first, last = occupancy_patch(
        eta_boxes, place_here, rows_dev + over_x, cols_dev + over_y, over_x, (own_planes,)
    )
    first_leg = [lax.ppermute(planes, "py", facing) for planes in mirror[1:]]
    mirror_zero = first_leg.pop(1)
    own_zero = own_planes[half:]
    middle_own = 0.5 * (own_zero + mirror_zero)
    payload = jnp.where(p == 0, middle_own, mirror_zero)
    pairs = [(0, middle)] + [(i, px - i) for i in range(1, middle)]
    from_zero = lax.ppermute(payload, "px", pairs)

    opposite = [(i, px - 1 - i) for i in range(px)]
    mirror = [lax.ppermute(planes, "px", opposite) for planes in first_leg]
    packs = -(-(half + 1) // slots)
    shape = (px, box_count, half, extent, span, length_x, cols_dev, over_y, slots, packs)
    after = (patch, mirror_zero, first_leg[-1], mirror[0])
    lines = box_rows(arrived, place, rows_forward, shape, py, after)
    along_x = exchange(lines, "py")
    first, last = from_behind(last, "px", 1), from_behind(first, "px", -1)
    first_gain = own_planes[:1] + jnp.where(p < middle, mirror[0][:1], from_zero)
    first_gain = jnp.where(p == middle, middle_own + from_zero, first_gain)
    conj_gain = jnp.where(p == middle, middle_own - from_zero, 0.0)
    gains = (first_gain[0], conj_gain[0])

    if cols_dev % LANES:
        along_x, packs = without_packs(along_x, half + 1, slots, over_y, py), 0
    me = lax.axis_index("py").astype(jnp.int32).reshape(1)
    pieces = []
    for k in range(chunks):
        lines = grid_columns(
            me,
            along_x,
            size,
            half,
            own_planes,
            k * size,
            mirror[k],
            gains if k == 0 else None,
            cols_forward,
            cols_inverse,
            slots,
            over_y,
            packs,
            (lines,) if k else (),
        )
        back = lines
        if cols_dev % LANES:
            lines = lines.reshape(2, size, kx_rows, py, cols_dev)
            lines = [exchange(jnp.transpose(lines, (3, 0, 1, 2, 4)), "py")]
        else:
            lines = send_round(lines, "py")
        if k == 0:
            patch, first, last = join_rows(patch, first, last, over_y, (back,))
        lines = back_rows(me, lines, rows_inverse, px, () if k else (patch, mirror[-1]))
        pieces.append(exchange(lines, "px"))
    first, last = from_behind(last, "py", 1), from_behind(first, "py", -1)

    window = patch.at[:, :over_y].add(first).at[:, cols_dev:].add(last)
    zero = jnp.zeros((), jnp.int32)
    results = []
    for b in range(box_count):
        position = (start_x[b], start_y[b], zero)
        total = lax.dynamic_slice(window, position, eta_boxes.shape[1:])
        results.append(advance(eta_boxes[b], total))
    base = jnp.stack(results)

    rows = back_depth(pieces, depth_inverse, (base,), over_x)
    potential = back_depth(pieces, depth_inverse, (rows,))
    pieces = potential_pieces(potential, rows, over_x, over_y)
    return (apply_potential(place_here, weights, base, eta_boxes, pieces), potential)


def solution(mesh):
    in_specs = (
        P(("px", "py"), None, None, None),
        P(("px", "py"), None),
        P(("px", "py")),
        P(),
        P("px", "py", None),
    )
    out_specs = (P(("px", "py"), None, None, None), P("px", "py", None))
    return jax.shard_map(
        on_device, mesh=mesh, in_specs=in_specs, out_specs=out_specs, check_vma=False
    )
```

```python
import functools
import math

import jax
import jax.numpy as jnp
import ml_dtypes
import numpy as np
from jax import lax
from jax.experimental import pallas as pl
from jax.experimental.pallas import tpu as pltpu
from jax.sharding import PartitionSpec as P

STEP = 8
LANES = 128
RADIX = 3

rate_step = 0.2
gradient_coef = 0.1
coupling = 1.5

F32 = jnp.float32
BF16 = jnp.bfloat16
MIB = 1 << 20


def from_behind(shard, axis, by):
    peers = lax.axis_size(axis)
    return lax.ppermute(shard, axis, [(i, (i + by) % peers) for i in range(peers)])


def laplace(values):
    padded = jnp.pad(values, ((1, 1), (1, 1), (0, 0)))
    beside_all = padded[2:, 1:-1] + padded[:-2, 1:-1] + padded[1:-1, 2:] + padded[1:-1, :-2]
    beside_all = beside_all + jnp.roll(values, 1, axis=2) + jnp.roll(values, -1, axis=2)
    return beside_all - 6.0 * values


def advance(order_param, occupancy):
    square = order_param * order_param
    force = order_param * square - order_param + 2.0 * coupling * order_param * (occupancy - square)
    force = force - gradient_coef * laplace(order_param)
    return order_param - rate_step * force


def pair_of(table):
    high = table.astype(ml_dtypes.bfloat16)
    low = (table - high.astype(np.float64)).astype(ml_dtypes.bfloat16)
    return high, low


def angle_of(index, length):
    return (index % length) * (2.0 * math.pi / length)


def depth_tables(depth, owners, sizes, scale):
    own = depth // owners
    half = own // 2
    z = np.arange(depth)

    def rows_of(p, planes):
        forward, inverse = ([], []), ([], [])
        for t in planes:
            angles = angle_of((own * p + t + (1 if p < owners // 2 else 0)) * z, depth)
            c, s, factor = np.cos(angles), np.sin(angles), scale
            if p == owners // 2 and t == 0:
                s, factor = -np.ones(depth), 0.5 * scale
            forward[0].append(c)
            forward[1].append(-s)
            inverse[0].append(factor * c)
            inverse[1].append(-factor * s)
        return forward[0] + forward[1], inverse[0] + inverse[1]

    out = []
    for p in range(owners):
        out += rows_of(p, range(half))[0]
    back = []
    begin = 0
    for size in sizes:
        for p in range(owners):
            back += rows_of(p, range(begin, begin + size))[1]
        begin += size
    return pair_of(np.array(out)), pair_of(np.array(back))


def row_tables(length):
    part = length // RADIX
    m = np.arange(part)
    forward, inverse = [], []
    for l in range(RADIX):
        angles = angle_of(m[:, None] * (RADIX * m[None, :] + l), length)
        c, s = np.cos(angles), np.sin(angles)
        forward.append(np.block([[c, s], [-s, c]]))
        c, s = c.T, s.T
        inverse.append(np.block([[c, -s], [s, c]]))
    return pair_of(np.array(forward)), pair_of(np.array(inverse))


def column_tables(length):
    part = length // 2
    m = np.arange(part)
    forward, inverse = [], []
    for parity in range(2):
        angles = angle_of(m[:, None] * (2 * m[None, :] + parity), length)
        c, s = np.cos(angles), np.sin(angles)
        forward.append(np.block([[c, -s], [s, c]]))
        c, s = c.T, s.T
        inverse.append(np.block([[c, s], [-s, c]]))
    return pair_of(np.array(forward)), pair_of(np.array(inverse))


def mirror_tables(rows, length):
    part = length // 2
    m = np.arange(part)
    order = np.concatenate([2 * m, 2 * m + 1])
    straight = np.zeros((length, length))
    straight[order, np.arange(length)] = 1.0
    mirrored = np.zeros((length, length))
    mirrored[(length - order) % length, np.arange(length)] = 1.0
    flip = np.zeros((rows, rows))
    i = np.arange(1, rows)
    flip[i, rows - i] = 1.0
    as_bf16 = lambda table: table.astype(ml_dtypes.bfloat16)
    return as_bf16(straight), as_bf16(mirrored), as_bf16(flip)


def halves(values):
    high = values.astype(BF16)
    return high, (values - high.astype(F32)).astype(BF16)


def dot(a, b):
    return jnp.dot(a, b, preferred_element_type=F32)


def table_first(high, low, values):
    top, rest = halves(values)
    width = values.shape[1]
    if width % LANES == 0:
        both = dot(high, jnp.concatenate([top, rest], axis=1))
        both = both[:, :width] + both[:, width:]
    else:
        both = dot(high, top) + dot(high, rest)
    return both + dot(low, top)


def table_last(values, high, low):
    top, rest = halves(values)
    rows = values.shape[0]
    both = dot(jnp.concatenate([top, rest], axis=0), high)
    return both[:rows] + both[rows:] + dot(top, low)


def cost(*arrays):
    size = sum(math.prod(array.shape) * 4 for array in arrays)
    return pl.CostEstimate(flops=0, bytes_accessed=5 * size, transcendentals=0)


def params(mib):
    return pltpu.CompilerParams(vmem_limit_bytes=mib * MIB)


ANYWHERE = pl.BlockSpec(memory_space=pl.ANY)


def waiting(kernel, before, after):
    def body(*refs):
        kernel(*refs[:before], *refs[before + len(after) :])

    return body


def whole(array):
    rank = len(array.shape)
    return pl.BlockSpec(array.shape, lambda *_: (0,) * rank)


def depth_kernel(weights, place, eta, high, low, out):
    boxes, extent, span = eta.shape[0], eta.shape[1], eta.shape[2]
    owners = out.shape[0]
    planes = high.shape[0] // owners
    dims = (((1,), (1,)), ((), ()))
    for i in range(extent):
        rows = []
        for b in range(boxes):
            values = eta[b, i]
            rows.append(weights[b] * (values * values))
        field = jnp.concatenate(rows, axis=0)
        top, rest = halves(field)
        count = field.shape[0]
        both = lax.dot_general(
            high[...], jnp.concatenate([top, rest], axis=0), dims, preferred_element_type=F32
        )
        small = lax.dot_general(low[...], top, dims, preferred_element_type=F32)
        result = both[:, :count] + both[:, count:] + small
        for p in range(owners):
            out[p, pl.ds(i, planes, stride=extent), :] = result[p * planes : (p + 1) * planes]
    lane = lax.broadcasted_iota(jnp.int32, (STEP, boxes * span), 1)
    where_to = jnp.zeros(lane.shape, jnp.int32)
    for k in range(2 * boxes):
        where_to = jnp.where(lane == k, place[k], where_to)
    for p in range(owners):
        out[p, planes * extent :, :] = where_to.astype(F32)


def box_depth(eta_boxes, weights, place, tables, owners, after):
    high, low = tables
    boxes, extent, span, depth = eta_boxes.shape
    shape = (owners, high.shape[0] // owners * extent + STEP, boxes * span)
    return pl.pallas_call(
        waiting(depth_kernel, 5, after),
        out_shape=jax.ShapeDtypeStruct(shape, F32),
        in_specs=[
            pl.BlockSpec(memory_space=pltpu.SMEM),
            pl.BlockSpec(memory_space=pltpu.SMEM),
            whole(eta_boxes),
            whole(high),
            whole(low),
            *([ANYWHERE] * len(after)),
        ],
        out_specs=pl.BlockSpec(shape, lambda: (0, 0, 0)),
        compiler_params=params(24),
        cost_estimate=cost(eta_boxes, eta_boxes),
        name="box_depth",
    )(weights, place, eta_boxes, high, low, *after)


def rows_kernel(shape, place, boxes_re, boxes_im, high, low, out, lines, packed):
    owners, per_owner, half, extent, span, length, cols, over, slots, packs = shape
    step = pl.program_id(0)
    lane = lax.broadcasted_iota(jnp.int32, (extent, LANES), 1)
    side = lines.shape[0]

    @pl.when(step == 0)
    def _():
        packed[...] = jnp.zeros(packed.shape, F32)

    @pl.when((step <= half) & (step != 1))
    def _():
        lines[...] = jnp.zeros(lines.shape, F32)

        def add_owner(s, carry):
            values = (boxes_re[s], boxes_im[s])
            moved = []
            for b in range(per_owner):
                column = place[2 * (s * per_owner + b) + 1]
                inside = (lane >= b * span) & (lane < (b + 1) * span)
                shift = lax.rem(column + (LANES - b * span), LANES)
                for v in values:
                    moved.append(pltpu.roll(jnp.where(inside, v, 0.0), shift, axis=1))
            for b in range(per_owner):
                at = 2 * (s * per_owner + b)
                where_to = pl.ds(pl.multiple_of(place[at], STEP), extent)
                here = lane >= place[at + 1]
                for ri in range(2):
                    value = moved[2 * b + ri]
                    lines[0, ri, where_to, :] += jnp.where(here, value, 0.0)
                    if side > 1:
                        lines[1, ri, where_to, :] += jnp.where(here, 0.0, value)
            return carry

        lax.fori_loop(0, owners, add_owner, 0, unroll=4)
        lines[:, :, :extent, :] += lines[:, :, length:, :]

    sign = jnp.where(step == 1, -1.0, 1.0).astype(F32)

    for k in range(half + 1):
        slot = half if k == 1 else max(k - 1, 0)

        @pl.when(step == k)
        def _(slot=slot):
            lanes_all = lax.broadcasted_iota(jnp.int32, (length, LANES), 1)
            for ri in range(2):
                beyond = lines[side - 1, ri, :length, :]
                if side == 1:
                    beyond = jnp.where(lanes_all >= cols, beyond, 0.0)
                shift = ((slot % slots) * over - (cols % LANES)) % LANES
                if shift:
                    beyond = pltpu.roll(beyond, shift, axis=1)
                packed[slot // slots, ri] += beyond * (sign if ri else 1.0)

    for k in range(packs):

        @pl.when(step == half + 1 + k)
        def _(k=k):
            lines[0, :, :length, :] = packed[k]

    part = length // RADIX
    terms = []
    for l in range(RADIX):
        take = pl.ds(l, part, stride=RADIX)
        values = jnp.concatenate([lines[0, 0, take, :], lines[0, 1, take, :] * sign], axis=0)
        terms.append(table_first(high[l], low[l], values))
    real, imag = [v[:part] for v in terms], [v[part:] for v in terms]
    root = math.sqrt(0.75)
    sum_re, sum_im = real[1] + real[2], imag[1] + imag[2]
    dif_re, dif_im = root * (real[1] - real[2]), root * (imag[1] - imag[2])
    mid_re, mid_im = real[0] - 0.5 * sum_re, imag[0] - 0.5 * sum_im
    result_re = jnp.concatenate([real[0] + sum_re, mid_re + dif_im, mid_re - dif_im], axis=0)
    result_im = jnp.concatenate([imag[0] + sum_im, mid_im - dif_re, mid_im + dif_re], axis=0)
    block = (out.shape[0], out.shape[3], LANES)
    out[:, 0, 0] = result_re.reshape(block)[:, :, :cols]
    out[:, 1, 0] = result_im.reshape(block)[:, :, :cols]


def box_rows(pieces, place, tables, shape, parts, after):
    owners, per_owner, half, extent, span, length, cols, over, slots, packs = shape
    high, low = tables
    planes = half + 1 + packs
    rows = length // parts
    side = -(-(cols + over) // LANES)

    def plane_in(k):
        return jnp.clip(k - 1, 0, half - 1)

    def plane_out(k, place):
        return (0, 0, jnp.where(k == 1, half, jnp.where(k > half, k, jnp.maximum(k - 1, 0))), 0, 0)

    return pl.pallas_call(
        waiting(functools.partial(rows_kernel, shape), 5, after),
        out_shape=jax.ShapeDtypeStruct((parts, 2, planes, rows, cols), F32),
        grid_spec=pltpu.PrefetchScalarGridSpec(
            num_scalar_prefetch=1,
            grid=(planes,),
            in_specs=[
                pl.BlockSpec((owners, extent, LANES), lambda k, place: (0, plane_in(k), 0)),
                pl.BlockSpec((owners, extent, LANES), lambda k, place: (0, half + plane_in(k), 0)),
                whole(high),
                whole(low),
                *([ANYWHERE] * len(after)),
            ],
            out_specs=pl.BlockSpec((parts, 2, 1, rows, cols), plane_out),
            scratch_shapes=[
                pltpu.VMEM((side, 2, length + extent, LANES), F32),
                pltpu.VMEM((packs, 2, length, LANES), F32),
            ],
        ),
        compiler_params=params(56),
        cost_estimate=cost(pieces, jax.ShapeDtypeStruct((parts, 2, planes, rows, cols), F32)),
        name="box_rows",
    )(place, pieces, pieces, high, low, *after)


def columns_kernel(slots, over, has_packs, has_conj, begin, half, counts, *refs):
    refs = list(refs)
    me = refs.pop(0)[0]
    main = refs.pop(0)
    pack = refs.pop(0) if has_packs else None
    conj = refs.pop(0) if has_conj else None
    conj_pack = refs.pop(0) if has_conj and has_packs else None
    own = refs.pop(0)
    mirrors = [refs.pop(0) for _ in counts]
    first_gain, conj_gain = (refs.pop(0), refs.pop(0)) if has_conj else (None, None)
    fwd_high, fwd_low, inv_high, inv_low = refs[:4]
    parts = main.shape[0]
    outs = refs[-2 - parts : -2]
    scratch, lines = refs[-2:]
    step = pl.program_id(0)
    rows, cols = main.shape[3], main.shape[4]
    half_length = fwd_high.shape[1] // 2

    def gathered(body, overhang, slot):
        pieces = []
        for ri in range(2):
            line = []
            for q in range(parts):
                piece = body[q, ri, 0]
                if has_packs:
                    lane = lax.broadcasted_iota(jnp.int32, piece.shape, 1)
                    shift = lax.rem(cols - over * slot, cols)
                    beyond = pltpu.roll(overhang[(q - 1) % parts, ri, 0], shift, axis=1)
                    piece = piece + jnp.where(lane < over, beyond, 0.0)
                line.append(piece)
            pieces.append(jnp.concatenate(line, axis=1) if parts > 1 else line[0])
        lower = [v[:, :half_length] for v in pieces]
        upper = [v[:, half_length:] for v in pieces]
        even = jnp.concatenate([a + b for a, b in zip(lower, upper)], axis=1)
        odd = jnp.concatenate([a - b for a, b in zip(lower, upper)], axis=1)
        return even, odd

    def forward(body, overhang, slot):
        even, odd = gathered(body, overhang, slot)
        return (
            table_last(even, fwd_high[0], fwd_low[0]),
            table_last(odd, fwd_high[1], fwd_low[1]),
        )

    def scaled(spectrum, gain):
        even, odd = spectrum
        left, right = gain[:, :half_length], gain[:, half_length:]
        left = jnp.concatenate([left, left], axis=1)
        right = jnp.concatenate([right, right], axis=1)
        return even * left, odd * right

    mirror = mirrors[0][0]
    for k in range(1, len(counts)):
        mirror = jnp.where(step >= sum(counts[:k]), mirrors[k][0], mirror)
    gain = own[0] + mirror
    if has_conj:
        gain = jnp.where(step == 0, first_gain[...], gain)
    even, odd = scaled(forward(main, pack, lax.rem(step + begin, slots)), gain)
    scratch[0] = even
    scratch[1] = odd

    if has_conj:

        @pl.when(step == 0)
        def _():
            even, odd = scaled(forward(conj, conj_pack, half % slots), conj_gain[...])
            scratch[0] += even
            scratch[1] += odd

    even = table_last(scratch[0], inv_high[0], inv_low[0])
    odd = table_last(scratch[1], inv_high[1], inv_low[1])
    lower, upper = even + odd, even - odd
    for ri in range(2):
        take = slice(ri * half_length, (ri + 1) * half_length)
        line = jnp.concatenate([lower[:, take], upper[:, take]], axis=1)
        for q in range(parts):
            lines[q] = line[:, q * cols : (q + 1) * cols]
        for r, out in enumerate(outs):
            out[ri, 0] = lines[lax.rem(me + r, parts)]


def grid_columns(me, arrived, count, half, own, begin, mirror, gains, forward, inverse, slots, over, packs, after):
    parts, _, planes, rows, cols = arrived.shape
    length = own.shape[2]
    has_packs, has_conj = packs > 0, gains is not None
    one = (parts, 2, 1, rows, cols)
    operands = [me, arrived]
    specs = [
        pl.BlockSpec(memory_space=pltpu.SMEM),
        pl.BlockSpec(one, lambda t: (0, 0, begin + t, 0, 0)),
    ]
    if has_packs:
        operands += [arrived]
        specs += [pl.BlockSpec(one, lambda t: (0, 0, half + 1 + (begin + t) // slots, 0, 0))]
    if has_conj:
        operands += [arrived]
        specs += [pl.BlockSpec(one, lambda t: (0, 0, half, 0, 0))]
        if has_packs:
            operands += [arrived]
            specs += [pl.BlockSpec(one, lambda t: (0, 0, half + 1 + half // slots, 0, 0))]
    operands += [own, *mirror]
    specs += [pl.BlockSpec((1, rows, length), lambda t: (begin + t, 0, 0))]
    counts = [m.shape[0] for m in mirror]
    for k, many in enumerate(counts):
        skip = sum(counts[:k])
        specs += [
            pl.BlockSpec(
                (1, rows, length),
                lambda t, skip=skip, many=many: (jnp.clip(t - skip, 0, many - 1), 0, 0),
            )
        ]
    fixed = [*(gains or ()), *forward, *inverse]
    return pl.pallas_call(
        functools.partial(columns_kernel, slots, over, has_packs, has_conj, begin, half, counts),
        out_shape=[jax.ShapeDtypeStruct((2, count, rows, cols), F32)] * parts,
        grid=(count,),
        in_specs=specs + [whole(t) for t in fixed] + [ANYWHERE] * len(after),
        out_specs=[pl.BlockSpec((2, 1, rows, cols), lambda t: (0, t, 0, 0))] * parts,
        scratch_shapes=[
            pltpu.VMEM((2, rows, length), F32),
            pltpu.VMEM((parts, rows, cols), F32),
        ],
        compiler_params=params(56),
        cost_estimate=cost(jax.ShapeDtypeStruct((parts, 6, count, rows, cols), F32)),
        name="grid_columns",
    )(*operands, *fixed, *after)


def back_rows_kernel(count, *refs):
    me = refs[0][0]
    bodies = refs[1 : 1 + count]
    high, low, out, lines = refs[1 + count :]
    parts, rows, cols = lines.shape[0], lines.shape[2], lines.shape[3]
    length = parts * rows
    part = length // RADIX
    owners, group = out.shape[0], out.shape[3] // RADIX
    if count == 1:
        lines[...] = bodies[0][:, :, 0]
    else:
        for r, body in enumerate(bodies):
            lines[lax.rem(me - r + parts, parts)] = body[:, 0]
    real = lines[:, 0].reshape(length, cols)
    imag = lines[:, 1].reshape(length, cols)
    real = [real[t * part : (t + 1) * part] for t in range(RADIX)]
    imag = [imag[t * part : (t + 1) * part] for t in range(RADIX)]
    root = math.sqrt(0.75)
    sum_re, sum_im = real[1] + real[2], imag[1] + imag[2]
    dif_re, dif_im = root * (real[1] - real[2]), root * (imag[1] - imag[2])
    mid_re, mid_im = real[0] - 0.5 * sum_re, imag[0] - 0.5 * sum_im
    terms = [
        (real[0] + sum_re, imag[0] + sum_im),
        (mid_re - dif_im, mid_im + dif_re),
        (mid_re + dif_im, mid_im - dif_re),
    ]
    for l in range(RADIX):
        result = table_first(high[l], low[l], jnp.concatenate(terms[l], axis=0))
        for ri in range(2):
            values = result[ri * part : (ri + 1) * part].reshape(owners, group, cols)
            out[:, ri, 0, l * group : (l + 1) * group, :] = values


def back_rows(me, bodies, tables, owners, after):
    high, low = tables
    half, rows, cols = bodies[0].shape[-3:]
    if len(bodies) == 1:
        parts = bodies[0].shape[0]
        spec = pl.BlockSpec((parts, 2, 1, rows, cols), lambda t: (0, 0, t, 0, 0))
    else:
        parts = len(bodies)
        spec = pl.BlockSpec((2, 1, rows, cols), lambda t: (0, t, 0, 0))
    length = parts * rows
    out = jax.ShapeDtypeStruct((owners, 2, half, length // owners, cols), F32)
    return pl.pallas_call(
        waiting(functools.partial(back_rows_kernel, len(bodies)), len(bodies) + 3, after),
        out_shape=out,
        grid=(half,),
        in_specs=[pl.BlockSpec(memory_space=pltpu.SMEM)]
        + [spec] * len(bodies)
        + [whole(high), whole(low)]
        + [ANYWHERE] * len(after),
        out_specs=pl.BlockSpec((owners, 2, 1, length // owners, cols), lambda t: (0, 0, t, 0, 0)),
        scratch_shapes=[pltpu.VMEM((parts, 2, rows, cols), F32)],
        compiler_params=params(56),
        cost_estimate=cost(out, out),
        name="back_rows",
    )(me, *bodies, high, low, *after)


def back_depth_kernel(chunks, *refs):
    bodies = refs[:chunks]
    high, low = refs[chunks : chunks + 2]
    out = refs[-1]
    group = out.shape[0]
    dims = (((0,), (0,)), ((), ()))
    for g in range(group):
        for l in range(RADIX):
            lines = [body[:, l, g, :] for body in bodies]
            values = jnp.concatenate(lines, axis=0) if chunks > 1 else lines[0]
            top, rest = halves(values)
            total = lax.dot_general(top, high[...], dims, preferred_element_type=F32)
            total += lax.dot_general(rest, high[...], dims, preferred_element_type=F32)
            total += lax.dot_general(top, low[...], dims, preferred_element_type=F32)
            out[g, l] = total


def back_depth(arrived, tables, after, only=None):
    high, low = tables
    chunks = len(arrived)
    depth = high.shape[1]
    rows, cols = arrived[0].shape[-2:]
    group = rows // RADIX
    take = group if only is None else only // RADIX
    bodies = [piece.reshape(-1, RADIX, group, cols) for piece in arrived]
    blocks = [(body.shape[0], RADIX, STEP, cols) for body in bodies]
    found = pl.pallas_call(
        functools.partial(back_depth_kernel, chunks),
        out_shape=jax.ShapeDtypeStruct((take, RADIX, cols, depth), F32),
        grid=(take // STEP,),
        in_specs=[pl.BlockSpec(block, lambda g: (0, 0, g, 0)) for block in blocks]
        + [whole(high), whole(low)]
        + [ANYWHERE] * len(after),
        out_specs=pl.BlockSpec((STEP, RADIX, cols, depth), lambda g: (g, 0, 0, 0)),
        compiler_params=params(56),
        cost_estimate=cost(*bodies, *bodies),
        name="back_depth",
    )(*bodies, high, low, *after)
    return found.reshape(take * RADIX, cols, depth)


def mirror_kernel(index, other, edge, mirrored, flip, out):
    rows, length = other.shape[1], other.shape[2]
    top, rest = halves(other[0])
    turned = dot(flip[...], jnp.concatenate([top, rest], axis=1))
    edge_top, edge_rest = halves(edge[0])
    row = lax.broadcasted_iota(jnp.int32, (rows, length), 0)
    top = jnp.where(row == 0, edge_top.astype(F32), turned[:, :length])
    rest = jnp.where(row == 0, edge_rest.astype(F32), turned[:, length:])
    both = dot(jnp.concatenate([top, rest], axis=0).astype(BF16), mirrored[...])
    out[0] = both[:rows] + both[rows:]


def mirror_planes(green, edge, index, mirrored, flip, after):
    rows, length = green.shape[1:]
    block = (1, rows, length)
    count = index.shape[0]
    return pl.pallas_call(
        waiting(mirror_kernel, 5, after),
        out_shape=jax.ShapeDtypeStruct((count, rows, length), F32),
        grid_spec=pltpu.PrefetchScalarGridSpec(
            num_scalar_prefetch=1,
            grid=(count,),
            in_specs=[
                pl.BlockSpec(block, lambda t, index: (index[t], 0, 0)),
                pl.BlockSpec((1, 1, length), lambda t, index: (index[t], 0, 0)),
                whole(mirrored),
                whole(flip),
                *([ANYWHERE] * len(after)),
            ],
            out_specs=pl.BlockSpec(block, lambda t, index: (t, 0, 0)),
        ),
        compiler_params=params(16),
        cost_estimate=cost(jax.ShapeDtypeStruct((count, rows, length), F32)),
        name="mirror_planes",
    )(index, green, edge, mirrored, flip, *after)


def order_kernel(index, own, straight, out):
    rows = own.shape[1]
    top, rest = halves(own[0])
    both = dot(jnp.concatenate([top, rest], axis=0), straight[...])
    out[0] = both[:rows] + both[rows:]


def order_planes(green, index, straight, after):
    rows, length = green.shape[1:]
    block = (1, rows, length)
    count = index.shape[0]
    return pl.pallas_call(
        waiting(order_kernel, 3, after),
        out_shape=jax.ShapeDtypeStruct((count, rows, length), F32),
        grid_spec=pltpu.PrefetchScalarGridSpec(
            num_scalar_prefetch=1,
            grid=(count,),
            in_specs=[
                pl.BlockSpec(block, lambda t, index: (index[t], 0, 0)),
                whole(straight),
                *([ANYWHERE] * len(after)),
            ],
            out_specs=pl.BlockSpec(block, lambda t, index: (t, 0, 0)),
        ),
        compiler_params=params(16),
        cost_estimate=cost(jax.ShapeDtypeStruct((count, rows, length), F32)),
        name="order_planes",
    )(index, green, straight, *after)


def edges_of(body, axis, first, last):
    over = first.shape[axis]
    if axis == 0:
        first[...] = body[:over]
        last[...] = body[body.shape[0] - over :]
    else:
        first[...] = body[:, :over, :]
        last[...] = body[:, body.shape[1] - over :, :]


def patch_kernel(place, eta, out, first, last):
    boxes, extent, span = eta.shape[0], eta.shape[1], eta.shape[2]
    out[...] = jnp.zeros(out.shape, F32)
    for b in range(boxes):
        row = place[2 * b]
        columns = pl.ds(pl.multiple_of(place[2 * b + 1], STEP), span)

        def add_row(i, carry, b=b, row=row, columns=columns):
            values = eta[b, i]
            out[row + i, columns, :] += values * values
            return carry

        lax.fori_loop(0, extent, add_row, 0, unroll=4)
    edges_of(out, 0, first, last)


def occupancy_patch(eta_boxes, place, rows, cols, over, after):
    depth = eta_boxes.shape[3]
    shapes = [(rows, cols, depth), (over, cols, depth), (over, cols, depth)]
    return pl.pallas_call(
        waiting(patch_kernel, 2, after),
        out_shape=[jax.ShapeDtypeStruct(shape, F32) for shape in shapes],
        in_specs=[pl.BlockSpec(memory_space=pltpu.SMEM), whole(eta_boxes)]
        + [ANYWHERE] * len(after),
        out_specs=[pl.BlockSpec(shape, lambda: (0, 0, 0)) for shape in shapes],
        compiler_params=params(32),
        cost_estimate=cost(eta_boxes),
        name="occupancy_patch",
    )(place, eta_boxes, *after)


def join_rows_kernel(body, behind, ahead, out, first, last):
    step, steps = pl.program_id(0), pl.num_programs(0)
    near = behind.shape[0] // out.shape[0]
    out[...] = body[...]
    count = out.shape[0]

    @pl.when(step < near)
    def _():
        out[...] += behind[pl.ds(step * count, count)]

    @pl.when(step >= steps - near)
    def _():
        out[...] += ahead[pl.ds((step - steps + near) * count, count)]

    edges_of(out, 1, first, last)


def join_rows(patch, behind, ahead, over, after):
    rows, cols, depth = patch.shape
    spec = pl.BlockSpec((STEP, cols, depth), lambda r: (r, 0, 0))
    side = pl.BlockSpec((STEP, over, depth), lambda r: (r, 0, 0))
    edge = jax.ShapeDtypeStruct((rows, over, depth), F32)
    return pl.pallas_call(
        waiting(join_rows_kernel, 3, after),
        out_shape=[jax.ShapeDtypeStruct(patch.shape, F32), edge, edge],
        grid=(rows // STEP,),
        in_specs=[spec, whole(behind), whole(ahead)] + [ANYWHERE] * len(after),
        out_specs=[spec, side, side],
        compiler_params=params(24),
        cost_estimate=cost(patch),
        name="join_rows",
    )(patch, behind, ahead, *after)


def apply_kernel(inside, place, weights, base, eta, *refs):
    sources, out = refs[:-1], refs[-1]
    boxes, extent, span = eta.shape[0], eta.shape[1], eta.shape[2]
    rows, cols = inside
    out[...] = base[...]

    def one_box(b, carry):
        first, column = place[2 * b], place[2 * b + 1]
        factor = (-2.0 * rate_step) * weights[b]
        for i in range(0, extent, STEP):
            x = first + i
            for j in range(0, span, STEP):
                y = pl.multiple_of(column + j, STEP)
                places = [
                    ((x < rows) & (y < cols), x, y),
                    ((x < rows) & (y >= cols), x, y - cols),
                    ((x >= rows) & (y < cols), x - rows, y),
                    ((x >= rows) & (y >= cols), x - rows, y - cols),
                ]
                places = places[:1] if len(sources) == 1 else places[1:]
                for source, (take, at_x, at_y) in zip(sources, places):

                    @pl.when(take)
                    def _(source=source, i=i, j=j, at_x=at_x, at_y=pl.multiple_of(at_y, STEP)):
                        mu = source[pl.ds(at_x, STEP), pl.ds(at_y, STEP), :]
                        here = (b, pl.ds(i, STEP), pl.ds(j, STEP), slice(None))
                        out[here] += factor * eta[here] * mu

        return carry

    lax.fori_loop(0, boxes, one_box, 0)


def apply_potential(place, weights, base, eta_boxes, sources, inside):
    arrays = [base, eta_boxes, *sources]
    smem = pl.BlockSpec(memory_space=pltpu.SMEM)
    return pl.pallas_call(
        functools.partial(apply_kernel, inside),
        out_shape=jax.ShapeDtypeStruct(eta_boxes.shape, F32),
        in_specs=[smem, smem] + [whole(v) for v in arrays],
        out_specs=whole(eta_boxes),
        compiler_params=params(36),
        cost_estimate=cost(eta_boxes, eta_boxes),
        name="apply_potential",
    )(place, weights, *arrays)


def halved(count):
    return [count // 2, count - count // 2] if count > 1 else [1]


def exchange(shard, axis):
    return lax.all_to_all(shard, axis, split_axis=0, concat_axis=0, tiled=True)


def send_round(lines, axis):
    return [lines[0]] + [from_behind(lines[r], axis, r) for r in range(1, len(lines))]


def potential_pieces(field, rows, over_x, over_y):
    px, py = lax.axis_size("px"), lax.axis_size("py")
    below = from_behind(rows, "px", -1)
    right = from_behind(field[:, :over_y], "py", -1)
    pairs = [
        (a * py + b, ((a - 1) % px) * py + (b - 1) % py) for a in range(px) for b in range(py)
    ]
    corner = lax.ppermute(rows[:, :over_y], ("px", "py"), pairs)
    return right, below, corner


def without_packs(along_x, count, slots, over, parts):
    body = count
    shifted = jnp.roll(along_x[:, :, body:], 1, axis=0)
    pieces = []
    for k in range(body):
        at = (k % slots) * over
        pieces.append(shifted[:, :, k // slots, :, at : at + over])
    body = along_x[:, :, :body].at[..., :over].add(jnp.stack(pieces, axis=2))
    body = jnp.transpose(body, (1, 2, 3, 0, 4))
    return body.reshape((1,) + body.shape[:3] + (-1,))


def on_device(eta_boxes, corners, grain_ids, misfit, green):
    px, py = lax.axis_size("px"), lax.axis_size("py")
    p = lax.axis_index("px")
    middle = px // 2
    box_count, extent, span, depth = eta_boxes.shape
    own, kx_rows, length_y = green.shape
    length_x = kx_rows * py
    rows_dev, cols_dev = length_x // px, length_y // py
    over_x, over_y = extent - STEP, span - STEP
    half = own // 2
    sizes = halved(half)
    begins = [sum(sizes[:k]) for k in range(len(sizes))]
    pieces = [halved(sizes[0]), *([size] for size in sizes[1:])]
    slots = cols_dev // over_y
    first_x = corners[:, 0] * STEP
    start_x = first_x - p * rows_dev
    start_y = corners[:, 1] * STEP - lax.axis_index("py") * cols_dev
    place_here = jnp.stack([start_x, start_y], axis=1).reshape(-1)
    variant = jnp.arange(misfit.shape[0], dtype=jnp.int32)
    weights = jnp.sum(
        jnp.where(grain_ids[:, None] == variant[None, :], misfit[None, :], 0.0), axis=1
    )
    scale = 1.0 / (length_x * length_y * depth)
    depth_forward, depth_inverse = depth_tables(depth, px, sizes, scale)
    rows_forward, rows_inverse = row_tables(length_x)
    cols_forward, cols_inverse = column_tables(length_y)
    straight, mirrored, flip = mirror_tables(kx_rows, length_y)

    edge = from_behind(green[:, :1, :], "py", -1)
    place_send = jnp.stack([first_x, start_y], axis=1).reshape(-1)
    spectra = box_depth(eta_boxes, weights, place_send, depth_forward, px, ())
    arrived = exchange(spectra, "px")
    place = arrived[:, -STEP, : 2 * box_count].astype(jnp.int32).reshape(-1)

    lower = (p < middle).astype(jnp.int32)
    t = jnp.arange(half, dtype=jnp.int32)
    facing = [(i, py - 1 - i) for i in range(py)]
    zero_index = jnp.zeros((1,), jnp.int32)
    index = jnp.minimum(own - 1 - t + lower, own - 1)
    indices = jnp.split(index, np.cumsum(sum(pieces, []))[:-1].tolist())
    indices[0] = jnp.concatenate([zero_index, indices[0]])
    own_zero = order_planes(green, zero_index, straight, (spectra,))
    mirror = [own_zero]
    for which in indices:
        mirror.append(mirror_planes(green, edge, which, mirrored, flip, (mirror[-1],)))
    own_planes = order_planes(green, t + lower, straight, (mirror[-1],))
    patch, first, last = occupancy_patch(
        eta_boxes, place_here, rows_dev + over_x, cols_dev + over_y, over_x, (own_planes,)
    )
    first_leg = [lax.ppermute(planes, "py", facing) for planes in mirror[1:]]
    mirror_zero, first_leg[0] = first_leg[0][:1], first_leg[0][1:]
    middle_own = 0.5 * (own_zero + mirror_zero)
    payload = jnp.where(p == 0, middle_own, mirror_zero)
    pairs = [(0, middle)] + [(i, px - i) for i in range(1, middle)]
    from_zero = lax.ppermute(payload, "px", pairs)

    opposite = [(i, px - 1 - i) for i in range(px)]
    mirror = [lax.ppermute(planes, "px", opposite) for planes in first_leg]
    packs = -(-(half + 1) // slots)
    shape = (px, box_count, half, extent, span, length_x, cols_dev, over_y, slots, packs)
    after = (patch, from_zero, *first_leg, mirror[0])
    lines = box_rows(arrived, place, rows_forward, shape, py, after)
    along_x = exchange(lines, "py")
    first, last = from_behind(last, "px", 1), from_behind(first, "px", -1)
    mirror = [mirror[: len(pieces[0])], *([m] for m in mirror[len(pieces[0]) :])]
    first_gain = own_planes[:1] + jnp.where(p < middle, mirror[0][0][:1], from_zero)
    first_gain = jnp.where(p == middle, middle_own + from_zero, first_gain)
    conj_gain = jnp.where(p == middle, middle_own - from_zero, 0.0)
    gains = (first_gain[0], conj_gain[0])

    if cols_dev % LANES:
        along_x, packs = without_packs(along_x, half + 1, slots, over_y, py), 0
    me = lax.axis_index("py").astype(jnp.int32).reshape(1)
    arrays = []
    for k, size in enumerate(sizes):
        lines = grid_columns(
            me,
            along_x,
            size,
            half,
            own_planes,
            begins[k],
            mirror[k],
            gains if k == 0 else None,
            cols_forward,
            cols_inverse,
            slots,
            over_y,
            packs,
            (lines,) if k else (),
        )
        back = lines[0]
        if cols_dev % LANES:
            lines = lines[0].reshape(2, size, kx_rows, py, cols_dev)
            lines = [exchange(jnp.transpose(lines, (3, 0, 1, 2, 4)), "py")]
        else:
            lines = send_round(lines, "py")
        if k == 0:
            patch, first, last = join_rows(patch, first, last, over_y, (back,))
        lines = back_rows(me, lines, rows_inverse, px, () if k else (patch, *sum(mirror, [])))
        arrays.append(exchange(lines, "px"))
    first, last = from_behind(last, "py", 1), from_behind(first, "py", -1)

    window = patch.at[:, :over_y].add(first).at[:, cols_dev:].add(last)
    zero = jnp.zeros((), jnp.int32)
    results = []
    for b in range(box_count):
        position = (start_x[b], start_y[b], zero)
        total = lax.dynamic_slice(window, position, eta_boxes.shape[1:])
        results.append(advance(eta_boxes[b], total))
    base = jnp.stack(results)

    rows = back_depth(arrays, depth_inverse, (base,), over_x)
    potential = back_depth(arrays, depth_inverse, (rows,))
    pieces = potential_pieces(potential, rows, over_x, over_y)
    inside = (rows_dev, cols_dev)
    base = apply_potential(place_here, weights, base, eta_boxes, [potential], inside)
    return (apply_potential(place_here, weights, base, eta_boxes, pieces, inside), potential)


def solution(mesh):
    in_specs = (
        P(("px", "py"), None, None, None),
        P(("px", "py"), None),
        P(("px", "py")),
        P(),
        P("px", "py", None),
    )
    out_specs = (P(("px", "py"), None, None, None), P("px", "py", None))
    return jax.shard_map(
        on_device, mesh=mesh, in_specs=in_specs, out_specs=out_specs, check_vma=False
    )
```

```python
import functools
import math

import jax
import jax.numpy as jnp
import ml_dtypes
import numpy as np
from jax import lax
from jax.experimental import pallas as pl
from jax.experimental.pallas import tpu as pltpu
from jax.sharding import PartitionSpec as P

STEP = 8
LANES = 128
RADIX = 3

rate_step = 0.2
gradient_coef = 0.1
coupling = 1.5

F32 = jnp.float32
BF16 = jnp.bfloat16
MIB = 1 << 20


def from_behind(shard, axis, by):
    peers = lax.axis_size(axis)
    return lax.ppermute(shard, axis, [(i, (i + by) % peers) for i in range(peers)])


def laplace(values):
    padded = jnp.pad(values, ((1, 1), (1, 1), (0, 0)))
    beside_all = padded[2:, 1:-1] + padded[:-2, 1:-1] + padded[1:-1, 2:] + padded[1:-1, :-2]
    beside_all = beside_all + jnp.roll(values, 1, axis=2) + jnp.roll(values, -1, axis=2)
    return beside_all - 6.0 * values


def advance(order_param, occupancy):
    square = order_param * order_param
    force = order_param * square - order_param + 2.0 * coupling * order_param * (occupancy - square)
    force = force - gradient_coef * laplace(order_param)
    return order_param - rate_step * force


def pair_of(table):
    high = table.astype(ml_dtypes.bfloat16)
    low = (table - high.astype(np.float64)).astype(ml_dtypes.bfloat16)
    return high, low


def angle_of(index, length):
    return (index % length) * (2.0 * math.pi / length)


def depth_tables(depth, owners, sizes, scale):
    own = depth // owners
    half = own // 2
    z = np.arange(depth)

    def rows_of(p, planes):
        forward, inverse = ([], []), ([], [])
        for t in planes:
            angles = angle_of((own * p + t + (1 if p < owners // 2 else 0)) * z, depth)
            c, s, factor = np.cos(angles), np.sin(angles), scale
            if p == owners // 2 and t == 0:
                s, factor = -np.ones(depth), 0.5 * scale
            forward[0].append(c)
            forward[1].append(-s)
            inverse[0].append(factor * c)
            inverse[1].append(-factor * s)
        return forward[0] + forward[1], inverse[0] + inverse[1]

    out = []
    for p in range(owners):
        out += rows_of(p, range(half))[0]
    back = []
    begin = 0
    for size in sizes:
        for p in range(owners):
            back += rows_of(p, range(begin, begin + size))[1]
        begin += size
    return pair_of(np.array(out)), pair_of(np.array(back))


def row_tables(length):
    part = length // RADIX
    m = np.arange(part)
    forward, inverse = [], []
    for l in range(RADIX):
        angles = angle_of(m[:, None] * (RADIX * m[None, :] + l), length)
        c, s = np.cos(angles), np.sin(angles)
        forward.append(np.stack([c, s - c, c + s]))
        inverse.append(np.stack([c.T, (s - c).T, (c + s).T]))
    return pair_of(np.array(forward)), pair_of(np.array(inverse))


def column_tables(length):
    part = length // 2
    m = np.arange(part)
    forward, inverse = [], []
    for parity in range(2):
        angles = angle_of(m[:, None] * (2 * m[None, :] + parity), length)
        c, s = np.cos(angles), np.sin(angles)
        forward.append(np.block([[c, -s], [s, c]]))
        c, s = c.T, s.T
        inverse.append(np.block([[c, s], [-s, c]]))
    return pair_of(np.array(forward)), pair_of(np.array(inverse))


def mirror_tables(rows, length):
    part = length // 2
    m = np.arange(part)
    order = np.concatenate([2 * m, 2 * m + 1])
    straight = np.zeros((length, length))
    straight[order, np.arange(length)] = 1.0
    mirrored = np.zeros((length, length))
    mirrored[(length - order) % length, np.arange(length)] = 1.0
    flip = np.zeros((rows, rows))
    i = np.arange(1, rows)
    flip[i, rows - i] = 1.0
    as_bf16 = lambda table: table.astype(ml_dtypes.bfloat16)
    return as_bf16(straight), as_bf16(mirrored), as_bf16(flip)


def halves(values):
    high = values.astype(BF16)
    return high, (values - high.astype(F32)).astype(BF16)


def dot(a, b):
    return jnp.dot(a, b, preferred_element_type=F32)


def table_first(high, low, values):
    top, rest = halves(values)
    width = values.shape[1]
    if width % LANES == 0:
        both = dot(high, jnp.concatenate([top, rest], axis=1))
        both = both[:, :width] + both[:, width:]
    else:
        both = dot(high, top) + dot(high, rest)
    return both + dot(low, top)


def table_last(values, high, low):
    top, rest = halves(values)
    rows = values.shape[0]
    both = dot(jnp.concatenate([top, rest], axis=0), high)
    return both[:rows] + both[rows:] + dot(top, low)


def cost(*arrays):
    size = sum(math.prod(array.shape) * 4 for array in arrays)
    return pl.CostEstimate(flops=0, bytes_accessed=5 * size, transcendentals=0)


def params(mib):
    return pltpu.CompilerParams(vmem_limit_bytes=mib * MIB)


ANYWHERE = pl.BlockSpec(memory_space=pl.ANY)


def waiting(kernel, before, after):
    def body(*refs):
        kernel(*refs[:before], *refs[before + len(after) :])

    return body


def whole(array):
    rank = len(array.shape)
    return pl.BlockSpec(array.shape, lambda *_: (0,) * rank)


def depth_kernel(weights, place, eta, high, low, out):
    boxes, extent, span = eta.shape[0], eta.shape[1], eta.shape[2]
    owners = out.shape[0]
    planes = high.shape[0] // owners
    dims = (((1,), (1,)), ((), ()))
    for i in range(extent):
        rows = []
        for b in range(boxes):
            values = eta[b, i]
            rows.append(weights[b] * (values * values))
        field = jnp.concatenate(rows, axis=0)
        top, rest = halves(field)
        count = field.shape[0]
        both = lax.dot_general(
            high[...], jnp.concatenate([top, rest], axis=0), dims, preferred_element_type=F32
        )
        small = lax.dot_general(low[...], top, dims, preferred_element_type=F32)
        result = both[:, :count] + both[:, count:] + small
        for p in range(owners):
            out[p, pl.ds(i, planes, stride=extent), :] = result[p * planes : (p + 1) * planes]
    lane = lax.broadcasted_iota(jnp.int32, (STEP, boxes * span), 1)
    where_to = jnp.zeros(lane.shape, jnp.int32)
    for k in range(2 * boxes):
        where_to = jnp.where(lane == k, place[k], where_to)
    for p in range(owners):
        out[p, planes * extent :, :] = where_to.astype(F32)


def box_depth(eta_boxes, weights, place, tables, owners, after):
    high, low = tables
    boxes, extent, span, depth = eta_boxes.shape
    shape = (owners, high.shape[0] // owners * extent + STEP, boxes * span)
    return pl.pallas_call(
        waiting(depth_kernel, 5, after),
        out_shape=jax.ShapeDtypeStruct(shape, F32),
        in_specs=[
            pl.BlockSpec(memory_space=pltpu.SMEM),
            pl.BlockSpec(memory_space=pltpu.SMEM),
            whole(eta_boxes),
            whole(high),
            whole(low),
            *([ANYWHERE] * len(after)),
        ],
        out_specs=pl.BlockSpec(shape, lambda: (0, 0, 0)),
        compiler_params=params(24),
        cost_estimate=cost(eta_boxes, eta_boxes),
        name="box_depth",
    )(weights, place, eta_boxes, high, low, *after)


def rows_kernel(shape, place, boxes_re, boxes_im, high, low, out, lines, packed):
    owners, per_owner, half, extent, span, length, cols, over, slots, packs = shape
    step = pl.program_id(0)
    lane = lax.broadcasted_iota(jnp.int32, (extent, LANES), 1)
    side = lines.shape[0]

    @pl.when(step == 0)
    def _():
        packed[...] = jnp.zeros(packed.shape, F32)

    @pl.when((step <= half) & (step != 1))
    def _():
        lines[...] = jnp.zeros(lines.shape, F32)

        def add_owner(s, carry):
            values = (boxes_re[s], boxes_im[s])
            moved = []
            for b in range(per_owner):
                column = place[2 * (s * per_owner + b) + 1]
                inside = (lane >= b * span) & (lane < (b + 1) * span)
                shift = lax.rem(column + (LANES - b * span), LANES)
                for v in values:
                    moved.append(pltpu.roll(jnp.where(inside, v, 0.0), shift, axis=1))
            for b in range(per_owner):
                at = 2 * (s * per_owner + b)
                where_to = pl.ds(pl.multiple_of(place[at], STEP), extent)
                here = lane >= place[at + 1]
                for ri in range(2):
                    value = moved[2 * b + ri]
                    lines[0, ri, where_to, :] += jnp.where(here, value, 0.0)
                    if side > 1:
                        lines[1, ri, where_to, :] += jnp.where(here, 0.0, value)
            return carry

        lax.fori_loop(0, owners, add_owner, 0, unroll=4)
        lines[:, :, :extent, :] += lines[:, :, length:, :]

    sign = jnp.where(step == 1, -1.0, 1.0).astype(F32)

    for k in range(half + 1):
        slot = half if k == 1 else max(k - 1, 0)

        @pl.when(step == k)
        def _(slot=slot):
            lanes_all = lax.broadcasted_iota(jnp.int32, (length, LANES), 1)
            for ri in range(2):
                beyond = lines[side - 1, ri, :length, :]
                if side == 1:
                    beyond = jnp.where(lanes_all >= cols, beyond, 0.0)
                shift = ((slot % slots) * over - (cols % LANES)) % LANES
                if shift:
                    beyond = pltpu.roll(beyond, shift, axis=1)
                packed[slot // slots, ri] += beyond * (sign if ri else 1.0)

    for k in range(packs):

        @pl.when(step == half + 1 + k)
        def _(k=k):
            lines[0, :, :length, :] = packed[k]

    part = length // RADIX
    terms = []
    for l in range(RADIX):
        take = pl.ds(l, part, stride=RADIX)
        re, im = lines[0, 0, take, :], lines[0, 1, take, :] * sign
        both = table_first(high[l, 0], low[l, 0], re + im)
        terms.append(
            (
                both + table_first(high[l, 1], low[l, 1], im),
                both - table_first(high[l, 2], low[l, 2], re),
            )
        )
    real, imag = [v[0] for v in terms], [v[1] for v in terms]
    root = math.sqrt(0.75)
    sum_re, sum_im = real[1] + real[2], imag[1] + imag[2]
    dif_re, dif_im = root * (real[1] - real[2]), root * (imag[1] - imag[2])
    mid_re, mid_im = real[0] - 0.5 * sum_re, imag[0] - 0.5 * sum_im
    result_re = jnp.concatenate([real[0] + sum_re, mid_re + dif_im, mid_re - dif_im], axis=0)
    result_im = jnp.concatenate([imag[0] + sum_im, mid_im - dif_re, mid_im + dif_re], axis=0)
    block = (out.shape[0], out.shape[3], LANES)
    out[:, 0, 0] = result_re.reshape(block)[:, :, :cols]
    out[:, 1, 0] = result_im.reshape(block)[:, :, :cols]


def box_rows(pieces, place, tables, shape, parts, after):
    owners, per_owner, half, extent, span, length, cols, over, slots, packs = shape
    high, low = tables
    planes = half + 1 + packs
    rows = length // parts
    side = -(-(cols + over) // LANES)

    def plane_in(k):
        return jnp.clip(k - 1, 0, half - 1)

    def plane_out(k, place):
        return (0, 0, jnp.where(k == 1, half, jnp.where(k > half, k, jnp.maximum(k - 1, 0))), 0, 0)

    return pl.pallas_call(
        waiting(functools.partial(rows_kernel, shape), 5, after),
        out_shape=jax.ShapeDtypeStruct((parts, 2, planes, rows, cols), F32),
        grid_spec=pltpu.PrefetchScalarGridSpec(
            num_scalar_prefetch=1,
            grid=(planes,),
            in_specs=[
                pl.BlockSpec((owners, extent, LANES), lambda k, place: (0, plane_in(k), 0)),
                pl.BlockSpec((owners, extent, LANES), lambda k, place: (0, half + plane_in(k), 0)),
                whole(high),
                whole(low),
                *([ANYWHERE] * len(after)),
            ],
            out_specs=pl.BlockSpec((parts, 2, 1, rows, cols), plane_out),
            scratch_shapes=[
                pltpu.VMEM((side, 2, length + extent, LANES), F32),
                pltpu.VMEM((packs, 2, length, LANES), F32),
            ],
        ),
        compiler_params=params(56),
        cost_estimate=cost(pieces, jax.ShapeDtypeStruct((parts, 2, planes, rows, cols), F32)),
        name="box_rows",
    )(place, pieces, pieces, high, low, *after)


def columns_kernel(slots, over, has_packs, has_conj, begin, half, counts, *refs):
    refs = list(refs)
    me = refs.pop(0)[0]
    main = refs.pop(0)
    pack = refs.pop(0) if has_packs else None
    conj = refs.pop(0) if has_conj else None
    conj_pack = refs.pop(0) if has_conj and has_packs else None
    own = refs.pop(0)
    mirrors = [refs.pop(0) for _ in counts]
    first_gain, conj_gain = (refs.pop(0), refs.pop(0)) if has_conj else (None, None)
    fwd_high, fwd_low, inv_high, inv_low = refs[:4]
    parts = main.shape[0]
    outs = refs[-2 - parts : -2]
    scratch, lines = refs[-2:]
    step = pl.program_id(0)
    rows, cols = main.shape[3], main.shape[4]
    half_length = fwd_high.shape[1] // 2

    def gathered(body, overhang, slot):
        pieces = []
        for ri in range(2):
            line = []
            for q in range(parts):
                piece = body[q, ri, 0]
                if has_packs:
                    lane = lax.broadcasted_iota(jnp.int32, piece.shape, 1)
                    shift = lax.rem(cols - over * slot, cols)
                    beyond = pltpu.roll(overhang[(q - 1) % parts, ri, 0], shift, axis=1)
                    piece = piece + jnp.where(lane < over, beyond, 0.0)
                line.append(piece)
            pieces.append(jnp.concatenate(line, axis=1) if parts > 1 else line[0])
        lower = [v[:, :half_length] for v in pieces]
        upper = [v[:, half_length:] for v in pieces]
        even = jnp.concatenate([a + b for a, b in zip(lower, upper)], axis=1)
        odd = jnp.concatenate([a - b for a, b in zip(lower, upper)], axis=1)
        return even, odd

    def forward(body, overhang, slot):
        even, odd = gathered(body, overhang, slot)
        return (
            table_last(even, fwd_high[0], fwd_low[0]),
            table_last(odd, fwd_high[1], fwd_low[1]),
        )

    def scaled(spectrum, gain):
        even, odd = spectrum
        left, right = gain[:, :half_length], gain[:, half_length:]
        left = jnp.concatenate([left, left], axis=1)
        right = jnp.concatenate([right, right], axis=1)
        return even * left, odd * right

    mirror = mirrors[0][0]
    for k in range(1, len(counts)):
        mirror = jnp.where(step >= sum(counts[:k]), mirrors[k][0], mirror)
    gain = own[0] + mirror
    if has_conj:
        gain = jnp.where(step == 0, first_gain[...], gain)
    even, odd = scaled(forward(main, pack, lax.rem(step + begin, slots)), gain)
    scratch[0] = even
    scratch[1] = odd

    if has_conj:

        @pl.when(step == 0)
        def _():
            even, odd = scaled(forward(conj, conj_pack, half % slots), conj_gain[...])
            scratch[0] += even
            scratch[1] += odd

    even = table_last(scratch[0], inv_high[0], inv_low[0])
    odd = table_last(scratch[1], inv_high[1], inv_low[1])
    lower, upper = even + odd, even - odd
    for ri in range(2):
        take = slice(ri * half_length, (ri + 1) * half_length)
        line = jnp.concatenate([lower[:, take], upper[:, take]], axis=1)
        for q in range(parts):
            lines[q] = line[:, q * cols : (q + 1) * cols]
        for r, out in enumerate(outs):
            out[ri, 0] = lines[lax.rem(me + r, parts)]


def grid_columns(me, arrived, count, half, own, begin, mirror, gains, forward, inverse, slots, over, packs, after):
    parts, _, planes, rows, cols = arrived.shape
    length = own.shape[2]
    has_packs, has_conj = packs > 0, gains is not None
    one = (parts, 2, 1, rows, cols)
    operands = [me, arrived]
    specs = [
        pl.BlockSpec(memory_space=pltpu.SMEM),
        pl.BlockSpec(one, lambda t: (0, 0, begin + t, 0, 0)),
    ]
    if has_packs:
        operands += [arrived]
        specs += [pl.BlockSpec(one, lambda t: (0, 0, half + 1 + (begin + t) // slots, 0, 0))]
    if has_conj:
        operands += [arrived]
        specs += [pl.BlockSpec(one, lambda t: (0, 0, half, 0, 0))]
        if has_packs:
            operands += [arrived]
            specs += [pl.BlockSpec(one, lambda t: (0, 0, half + 1 + half // slots, 0, 0))]
    operands += [own, *mirror]
    specs += [pl.BlockSpec((1, rows, length), lambda t: (begin + t, 0, 0))]
    counts = [m.shape[0] for m in mirror]
    for k, many in enumerate(counts):
        skip = sum(counts[:k])
        specs += [
            pl.BlockSpec(
                (1, rows, length),
                lambda t, skip=skip, many=many: (jnp.clip(t - skip, 0, many - 1), 0, 0),
            )
        ]
    fixed = [*(gains or ()), *forward, *inverse]
    return pl.pallas_call(
        functools.partial(columns_kernel, slots, over, has_packs, has_conj, begin, half, counts),
        out_shape=[jax.ShapeDtypeStruct((2, count, rows, cols), F32)] * parts,
        grid=(count,),
        in_specs=specs + [whole(t) for t in fixed] + [ANYWHERE] * len(after),
        out_specs=[pl.BlockSpec((2, 1, rows, cols), lambda t: (0, t, 0, 0))] * parts,
        scratch_shapes=[
            pltpu.VMEM((2, rows, length), F32),
            pltpu.VMEM((parts, rows, cols), F32),
        ],
        compiler_params=params(56),
        cost_estimate=cost(jax.ShapeDtypeStruct((parts, 6, count, rows, cols), F32)),
        name="grid_columns",
    )(*operands, *fixed, *after)


def back_rows_kernel(count, *refs):
    me = refs[0][0]
    bodies = refs[1 : 1 + count]
    high, low, out, lines = refs[1 + count :]
    parts, rows, cols = lines.shape[0], lines.shape[2], lines.shape[3]
    length = parts * rows
    part = length // RADIX
    owners, group = out.shape[0], out.shape[3] // RADIX
    if count == 1:
        lines[...] = bodies[0][:, :, 0]
    else:
        for r, body in enumerate(bodies):
            lines[lax.rem(me - r + parts, parts)] = body[:, 0]
    real = lines[:, 0].reshape(length, cols)
    imag = lines[:, 1].reshape(length, cols)
    real = [real[t * part : (t + 1) * part] for t in range(RADIX)]
    imag = [imag[t * part : (t + 1) * part] for t in range(RADIX)]
    root = math.sqrt(0.75)
    sum_re, sum_im = real[1] + real[2], imag[1] + imag[2]
    dif_re, dif_im = root * (real[1] - real[2]), root * (imag[1] - imag[2])
    mid_re, mid_im = real[0] - 0.5 * sum_re, imag[0] - 0.5 * sum_im
    terms = [
        (real[0] + sum_re, imag[0] + sum_im),
        (mid_re - dif_im, mid_im + dif_re),
        (mid_re + dif_im, mid_im - dif_re),
    ]
    for l in range(RADIX):
        re, im = terms[l]
        both = table_first(high[l, 0], low[l, 0], re + im)
        result = (
            both - table_first(high[l, 2], low[l, 2], im),
            both + table_first(high[l, 1], low[l, 1], re),
        )
        for ri in range(2):
            values = result[ri].reshape(owners, group, cols)
            out[:, ri, 0, l * group : (l + 1) * group, :] = values


def back_rows(me, bodies, tables, owners, after):
    high, low = tables
    half, rows, cols = bodies[0].shape[-3:]
    if len(bodies) == 1:
        parts = bodies[0].shape[0]
        spec = pl.BlockSpec((parts, 2, 1, rows, cols), lambda t: (0, 0, t, 0, 0))
    else:
        parts = len(bodies)
        spec = pl.BlockSpec((2, 1, rows, cols), lambda t: (0, t, 0, 0))
    length = parts * rows
    out = jax.ShapeDtypeStruct((owners, 2, half, length // owners, cols), F32)
    return pl.pallas_call(
        waiting(functools.partial(back_rows_kernel, len(bodies)), len(bodies) + 3, after),
        out_shape=out,
        grid=(half,),
        in_specs=[pl.BlockSpec(memory_space=pltpu.SMEM)]
        + [spec] * len(bodies)
        + [whole(high), whole(low)]
        + [ANYWHERE] * len(after),
        out_specs=pl.BlockSpec((owners, 2, 1, length // owners, cols), lambda t: (0, 0, t, 0, 0)),
        scratch_shapes=[pltpu.VMEM((parts, 2, rows, cols), F32)],
        compiler_params=params(56),
        cost_estimate=cost(out, out),
        name="back_rows",
    )(me, *bodies, high, low, *after)


def back_depth_kernel(chunks, *refs):
    bodies = refs[:chunks]
    high, low = refs[chunks : chunks + 2]
    out = refs[-1]
    group = out.shape[0]
    dims = (((0,), (0,)), ((), ()))
    for g in range(group):
        for l in range(RADIX):
            lines = [body[:, l, g, :] for body in bodies]
            values = jnp.concatenate(lines, axis=0) if chunks > 1 else lines[0]
            top, rest = halves(values)
            total = lax.dot_general(top, high[...], dims, preferred_element_type=F32)
            total += lax.dot_general(rest, high[...], dims, preferred_element_type=F32)
            total += lax.dot_general(top, low[...], dims, preferred_element_type=F32)
            out[g, l] = total


def back_depth(arrived, tables, after, only=None):
    high, low = tables
    chunks = len(arrived)
    depth = high.shape[1]
    rows, cols = arrived[0].shape[-2:]
    group = rows // RADIX
    take = group if only is None else only // RADIX
    bodies = [piece.reshape(-1, RADIX, group, cols) for piece in arrived]
    blocks = [(body.shape[0], RADIX, STEP, cols) for body in bodies]
    found = pl.pallas_call(
        functools.partial(back_depth_kernel, chunks),
        out_shape=jax.ShapeDtypeStruct((take, RADIX, cols, depth), F32),
        grid=(take // STEP,),
        in_specs=[pl.BlockSpec(block, lambda g: (0, 0, g, 0)) for block in blocks]
        + [whole(high), whole(low)]
        + [ANYWHERE] * len(after),
        out_specs=pl.BlockSpec((STEP, RADIX, cols, depth), lambda g: (g, 0, 0, 0)),
        compiler_params=params(56),
        cost_estimate=cost(*bodies, *bodies),
        name="back_depth",
    )(*bodies, high, low, *after)
    return found.reshape(take * RADIX, cols, depth)


def mirror_kernel(index, other, edge, mirrored, flip, out):
    rows, length = other.shape[1], other.shape[2]
    top, rest = halves(other[0])
    turned = dot(flip[...], jnp.concatenate([top, rest], axis=1))
    edge_top, edge_rest = halves(edge[0])
    row = lax.broadcasted_iota(jnp.int32, (rows, length), 0)
    top = jnp.where(row == 0, edge_top.astype(F32), turned[:, :length])
    rest = jnp.where(row == 0, edge_rest.astype(F32), turned[:, length:])
    both = dot(jnp.concatenate([top, rest], axis=0).astype(BF16), mirrored[...])
    out[0] = both[:rows] + both[rows:]


def mirror_planes(green, edge, index, mirrored, flip, after):
    rows, length = green.shape[1:]
    block = (1, rows, length)
    count = index.shape[0]
    return pl.pallas_call(
        waiting(mirror_kernel, 5, after),
        out_shape=jax.ShapeDtypeStruct((count, rows, length), F32),
        grid_spec=pltpu.PrefetchScalarGridSpec(
            num_scalar_prefetch=1,
            grid=(count,),
            in_specs=[
                pl.BlockSpec(block, lambda t, index: (index[t], 0, 0)),
                pl.BlockSpec((1, 1, length), lambda t, index: (index[t], 0, 0)),
                whole(mirrored),
                whole(flip),
                *([ANYWHERE] * len(after)),
            ],
            out_specs=pl.BlockSpec(block, lambda t, index: (t, 0, 0)),
        ),
        compiler_params=params(16),
        cost_estimate=cost(jax.ShapeDtypeStruct((count, rows, length), F32)),
        name="mirror_planes",
    )(index, green, edge, mirrored, flip, *after)


def order_kernel(index, own, straight, out):
    rows = own.shape[1]
    top, rest = halves(own[0])
    both = dot(jnp.concatenate([top, rest], axis=0), straight[...])
    out[0] = both[:rows] + both[rows:]


def order_planes(green, index, straight, after):
    rows, length = green.shape[1:]
    block = (1, rows, length)
    count = index.shape[0]
    return pl.pallas_call(
        waiting(order_kernel, 3, after),
        out_shape=jax.ShapeDtypeStruct((count, rows, length), F32),
        grid_spec=pltpu.PrefetchScalarGridSpec(
            num_scalar_prefetch=1,
            grid=(count,),
            in_specs=[
                pl.BlockSpec(block, lambda t, index: (index[t], 0, 0)),
                whole(straight),
                *([ANYWHERE] * len(after)),
            ],
            out_specs=pl.BlockSpec(block, lambda t, index: (t, 0, 0)),
        ),
        compiler_params=params(16),
        cost_estimate=cost(jax.ShapeDtypeStruct((count, rows, length), F32)),
        name="order_planes",
    )(index, green, straight, *after)


def edges_of(body, axis, first, last):
    over = first.shape[axis]
    if axis == 0:
        first[...] = body[:over]
        last[...] = body[body.shape[0] - over :]
    else:
        first[...] = body[:, :over, :]
        last[...] = body[:, body.shape[1] - over :, :]


def patch_kernel(place, eta, out, first, last):
    boxes, extent, span = eta.shape[0], eta.shape[1], eta.shape[2]
    out[...] = jnp.zeros(out.shape, F32)
    for b in range(boxes):
        row = place[2 * b]
        columns = pl.ds(pl.multiple_of(place[2 * b + 1], STEP), span)

        def add_row(i, carry, b=b, row=row, columns=columns):
            values = eta[b, i]
            out[row + i, columns, :] += values * values
            return carry

        lax.fori_loop(0, extent, add_row, 0, unroll=4)
    edges_of(out, 0, first, last)


def occupancy_patch(eta_boxes, place, rows, cols, over, after):
    depth = eta_boxes.shape[3]
    shapes = [(rows, cols, depth), (over, cols, depth), (over, cols, depth)]
    return pl.pallas_call(
        waiting(patch_kernel, 2, after),
        out_shape=[jax.ShapeDtypeStruct(shape, F32) for shape in shapes],
        in_specs=[pl.BlockSpec(memory_space=pltpu.SMEM), whole(eta_boxes)]
        + [ANYWHERE] * len(after),
        out_specs=[pl.BlockSpec(shape, lambda: (0, 0, 0)) for shape in shapes],
        compiler_params=params(32),
        cost_estimate=cost(eta_boxes),
        name="occupancy_patch",
    )(place, eta_boxes, *after)


def join_rows_kernel(body, behind, ahead, out, first, last):
    step, steps = pl.program_id(0), pl.num_programs(0)
    near = behind.shape[0] // out.shape[0]
    out[...] = body[...]
    count = out.shape[0]

    @pl.when(step < near)
    def _():
        out[...] += behind[pl.ds(step * count, count)]

    @pl.when(step >= steps - near)
    def _():
        out[...] += ahead[pl.ds((step - steps + near) * count, count)]

    edges_of(out, 1, first, last)


def join_rows(patch, behind, ahead, over, after):
    rows, cols, depth = patch.shape
    spec = pl.BlockSpec((STEP, cols, depth), lambda r: (r, 0, 0))
    side = pl.BlockSpec((STEP, over, depth), lambda r: (r, 0, 0))
    edge = jax.ShapeDtypeStruct((rows, over, depth), F32)
    return pl.pallas_call(
        waiting(join_rows_kernel, 3, after),
        out_shape=[jax.ShapeDtypeStruct(patch.shape, F32), edge, edge],
        grid=(rows // STEP,),
        in_specs=[spec, whole(behind), whole(ahead)] + [ANYWHERE] * len(after),
        out_specs=[spec, side, side],
        compiler_params=params(24),
        cost_estimate=cost(patch),
        name="join_rows",
    )(patch, behind, ahead, *after)


def apply_kernel(inside, place, weights, base, eta, *refs):
    sources, out = refs[:-1], refs[-1]
    boxes, extent, span = eta.shape[0], eta.shape[1], eta.shape[2]
    rows, cols = inside
    out[...] = base[...]

    def one_box(b, carry):
        first, column = place[2 * b], place[2 * b + 1]
        factor = (-2.0 * rate_step) * weights[b]
        for i in range(0, extent, STEP):
            x = first + i
            for j in range(0, span, STEP):
                y = pl.multiple_of(column + j, STEP)
                places = [
                    ((x < rows) & (y < cols), x, y),
                    ((x < rows) & (y >= cols), x, y - cols),
                    ((x >= rows) & (y < cols), x - rows, y),
                    ((x >= rows) & (y >= cols), x - rows, y - cols),
                ]
                places = places[:1] if len(sources) == 1 else places[1:]
                for source, (take, at_x, at_y) in zip(sources, places):

                    @pl.when(take)
                    def _(source=source, i=i, j=j, at_x=at_x, at_y=pl.multiple_of(at_y, STEP)):
                        mu = source[pl.ds(at_x, STEP), pl.ds(at_y, STEP), :]
                        here = (b, pl.ds(i, STEP), pl.ds(j, STEP), slice(None))
                        out[here] += factor * eta[here] * mu

        return carry

    lax.fori_loop(0, boxes, one_box, 0)


def apply_potential(place, weights, base, eta_boxes, sources, inside):
    arrays = [base, eta_boxes, *sources]
    smem = pl.BlockSpec(memory_space=pltpu.SMEM)
    return pl.pallas_call(
        functools.partial(apply_kernel, inside),
        out_shape=jax.ShapeDtypeStruct(eta_boxes.shape, F32),
        in_specs=[smem, smem] + [whole(v) for v in arrays],
        out_specs=whole(eta_boxes),
        compiler_params=params(36),
        cost_estimate=cost(eta_boxes, eta_boxes),
        name="apply_potential",
    )(place, weights, *arrays)


def halved(count):
    return [count // 2, count - count // 2] if count > 1 else [1]


def exchange(shard, axis):
    return lax.all_to_all(shard, axis, split_axis=0, concat_axis=0, tiled=True)


def send_round(lines, axis):
    return [lines[0]] + [from_behind(lines[r], axis, r) for r in range(1, len(lines))]


def potential_pieces(field, rows, over_x, over_y):
    px, py = lax.axis_size("px"), lax.axis_size("py")
    below = from_behind(rows, "px", -1)
    right = from_behind(field[:, :over_y], "py", -1)
    pairs = [
        (a * py + b, ((a - 1) % px) * py + (b - 1) % py) for a in range(px) for b in range(py)
    ]
    corner = lax.ppermute(rows[:, :over_y], ("px", "py"), pairs)
    return right, below, corner


def without_packs(along_x, count, slots, over, parts):
    body = count
    shifted = jnp.roll(along_x[:, :, body:], 1, axis=0)
    pieces = []
    for k in range(body):
        at = (k % slots) * over
        pieces.append(shifted[:, :, k // slots, :, at : at + over])
    body = along_x[:, :, :body].at[..., :over].add(jnp.stack(pieces, axis=2))
    body = jnp.transpose(body, (1, 2, 3, 0, 4))
    return body.reshape((1,) + body.shape[:3] + (-1,))


def on_device(eta_boxes, corners, grain_ids, misfit, green):
    px, py = lax.axis_size("px"), lax.axis_size("py")
    p = lax.axis_index("px")
    middle = px // 2
    box_count, extent, span, depth = eta_boxes.shape
    own, kx_rows, length_y = green.shape
    length_x = kx_rows * py
    rows_dev, cols_dev = length_x // px, length_y // py
    over_x, over_y = extent - STEP, span - STEP
    half = own // 2
    sizes = halved(half)
    begins = [sum(sizes[:k]) for k in range(len(sizes))]
    pieces = [halved(sizes[0]), *([size] for size in sizes[1:])]
    slots = cols_dev // over_y
    first_x = corners[:, 0] * STEP
    start_x = first_x - p * rows_dev
    start_y = corners[:, 1] * STEP - lax.axis_index("py") * cols_dev
    place_here = jnp.stack([start_x, start_y], axis=1).reshape(-1)
    variant = jnp.arange(misfit.shape[0], dtype=jnp.int32)
    weights = jnp.sum(
        jnp.where(grain_ids[:, None] == variant[None, :], misfit[None, :], 0.0), axis=1
    )
    scale = 1.0 / (length_x * length_y * depth)
    depth_forward, depth_inverse = depth_tables(depth, px, sizes, scale)
    rows_forward, rows_inverse = row_tables(length_x)
    cols_forward, cols_inverse = column_tables(length_y)
    straight, mirrored, flip = mirror_tables(kx_rows, length_y)

    edge = from_behind(green[:, :1, :], "py", -1)
    place_send = jnp.stack([first_x, start_y], axis=1).reshape(-1)
    spectra = box_depth(eta_boxes, weights, place_send, depth_forward, px, ())
    arrived = exchange(spectra, "px")
    place = arrived[:, -STEP, : 2 * box_count].astype(jnp.int32).reshape(-1)

    lower = (p < middle).astype(jnp.int32)
    t = jnp.arange(half, dtype=jnp.int32)
    facing = [(i, py - 1 - i) for i in range(py)]
    zero_index = jnp.zeros((1,), jnp.int32)
    index = jnp.minimum(own - 1 - t + lower, own - 1)
    indices = jnp.split(index, np.cumsum(sum(pieces, []))[:-1].tolist())
    indices[0] = jnp.concatenate([zero_index, indices[0]])
    own_zero = order_planes(green, zero_index, straight, (spectra,))
    mirror = [own_zero]
    for which in indices:
        mirror.append(mirror_planes(green, edge, which, mirrored, flip, (mirror[-1],)))
    own_planes = order_planes(green, t + lower, straight, (mirror[-1],))
    patch, first, last = occupancy_patch(
        eta_boxes, place_here, rows_dev + over_x, cols_dev + over_y, over_x, (own_planes,)
    )
    first_leg = [lax.ppermute(planes, "py", facing) for planes in mirror[1:]]
    mirror_zero, first_leg[0] = first_leg[0][:1], first_leg[0][1:]
    middle_own = 0.5 * (own_zero + mirror_zero)
    payload = jnp.where(p == 0, middle_own, mirror_zero)
    pairs = [(0, middle)] + [(i, px - i) for i in range(1, middle)]
    from_zero = lax.ppermute(payload, "px", pairs)

    opposite = [(i, px - 1 - i) for i in range(px)]
    mirror = [lax.ppermute(planes, "px", opposite) for planes in first_leg]
    packs = -(-(half + 1) // slots)
    shape = (px, box_count, half, extent, span, length_x, cols_dev, over_y, slots, packs)
    after = (patch, from_zero, *first_leg, mirror[0])
    lines = box_rows(arrived, place, rows_forward, shape, py, after)
    along_x = exchange(lines, "py")
    first, last = from_behind(last, "px", 1), from_behind(first, "px", -1)
    mirror = [mirror[: len(pieces[0])], *([m] for m in mirror[len(pieces[0]) :])]
    first_gain = own_planes[:1] + jnp.where(p < middle, mirror[0][0][:1], from_zero)
    first_gain = jnp.where(p == middle, middle_own + from_zero, first_gain)
    conj_gain = jnp.where(p == middle, middle_own - from_zero, 0.0)
    gains = (first_gain[0], conj_gain[0])

    if cols_dev % LANES:
        along_x, packs = without_packs(along_x, half + 1, slots, over_y, py), 0
    me = lax.axis_index("py").astype(jnp.int32).reshape(1)
    arrays = []
    for k, size in enumerate(sizes):
        lines = grid_columns(
            me,
            along_x,
            size,
            half,
            own_planes,
            begins[k],
            mirror[k],
            gains if k == 0 else None,
            cols_forward,
            cols_inverse,
            slots,
            over_y,
            packs,
            (lines,) if k else (),
        )
        back = lines[0]
        if cols_dev % LANES:
            lines = lines[0].reshape(2, size, kx_rows, py, cols_dev)
            lines = [exchange(jnp.transpose(lines, (3, 0, 1, 2, 4)), "py")]
        else:
            lines = send_round(lines, "py")
        if k == 0:
            patch, first, last = join_rows(patch, first, last, over_y, (back,))
        lines = back_rows(me, lines, rows_inverse, px, () if k else (patch, *sum(mirror, [])))
        arrays.append(exchange(lines, "px"))
    first, last = from_behind(last, "py", 1), from_behind(first, "py", -1)

    window = patch.at[:, :over_y].add(first).at[:, cols_dev:].add(last)
    zero = jnp.zeros((), jnp.int32)
    results = []
    for b in range(box_count):
        position = (start_x[b], start_y[b], zero)
        total = lax.dynamic_slice(window, position, eta_boxes.shape[1:])
        results.append(advance(eta_boxes[b], total))
    base = jnp.stack(results)

    rows = back_depth(arrays, depth_inverse, (base,), over_x)
    potential = back_depth(arrays, depth_inverse, (rows,))
    pieces = potential_pieces(potential, rows, over_x, over_y)
    inside = (rows_dev, cols_dev)
    base = apply_potential(place_here, weights, base, eta_boxes, [potential], inside)
    return (apply_potential(place_here, weights, base, eta_boxes, pieces, inside), potential)


def solution(mesh):
    in_specs = (
        P(("px", "py"), None, None, None),
        P(("px", "py"), None),
        P(("px", "py")),
        P(),
        P("px", "py", None),
    )
    out_specs = (P(("px", "py"), None, None, None), P("px", "py", None))
    return jax.shard_map(
        on_device, mesh=mesh, in_specs=in_specs, out_specs=out_specs, check_vma=False
    )
```

```python
import functools
import math

import jax
import jax.numpy as jnp
import ml_dtypes
import numpy as np
from jax import lax
from jax.experimental import pallas as pl
from jax.experimental.pallas import tpu as pltpu
from jax.sharding import PartitionSpec as P

STEP = 8
LANES = 128
RADIX = 3

rate_step = 0.2
gradient_coef = 0.1
coupling = 1.5

F32 = jnp.float32
BF16 = jnp.bfloat16
MIB = 1 << 20


def from_behind(shard, axis, by):
    peers = lax.axis_size(axis)
    return lax.ppermute(shard, axis, [(i, (i + by) % peers) for i in range(peers)])


def laplace(values):
    padded = jnp.pad(values, ((1, 1), (1, 1), (0, 0)))
    beside_all = padded[2:, 1:-1] + padded[:-2, 1:-1] + padded[1:-1, 2:] + padded[1:-1, :-2]
    beside_all = beside_all + jnp.roll(values, 1, axis=2) + jnp.roll(values, -1, axis=2)
    return beside_all - 6.0 * values


def advance(order_param, occupancy):
    square = order_param * order_param
    force = order_param * square - order_param + 2.0 * coupling * order_param * (occupancy - square)
    force = force - gradient_coef * laplace(order_param)
    return order_param - rate_step * force


def pair_of(table):
    high = table.astype(ml_dtypes.bfloat16)
    low = (table - high.astype(np.float64)).astype(ml_dtypes.bfloat16)
    return high, low


def angle_of(index, length):
    return (index % length) * (2.0 * math.pi / length)


def depth_tables(depth, owners, sizes, scale):
    own = depth // owners
    half = own // 2
    z = np.arange(depth)

    def rows_of(p, planes):
        forward, inverse = ([], []), ([], [])
        for t in planes:
            angles = angle_of((own * p + t + (1 if p < owners // 2 else 0)) * z, depth)
            c, s, factor = np.cos(angles), np.sin(angles), scale
            if p == owners // 2 and t == 0:
                s, factor = -np.ones(depth), 0.5 * scale
            forward[0].append(c)
            forward[1].append(-s)
            inverse[0].append(factor * c)
            inverse[1].append(-factor * s)
        return forward[0] + forward[1], inverse[0] + inverse[1]

    out = []
    for p in range(owners):
        out += rows_of(p, range(half))[0]
    back = []
    begin = 0
    for size in sizes:
        for p in range(owners):
            back += rows_of(p, range(begin, begin + size))[1]
        begin += size
    return pair_of(np.array(out)), pair_of(np.array(back))


def row_tables(length):
    part = length // RADIX
    m = np.arange(part)
    forward, inverse = [], []
    for l in range(RADIX):
        angles = angle_of(m[:, None] * (RADIX * m[None, :] + l), length)
        c, s = np.cos(angles), np.sin(angles)
        forward.append(np.stack([c, s - c, c + s]))
        inverse.append(np.stack([c.T, (s - c).T, (c + s).T]))
    return pair_of(np.array(forward)), pair_of(np.array(inverse))


def column_tables(length):
    part = length // 2
    m = np.arange(part)
    forward, inverse = [], []
    for parity in range(2):
        angles = angle_of(m[:, None] * (2 * m[None, :] + parity), length)
        c, s = np.cos(angles), np.sin(angles)
        forward.append(np.stack([c, s - c, c + s]))
        inverse.append(np.stack([c.T, (s - c).T, (c + s).T]))
    return pair_of(np.array(forward)), pair_of(np.array(inverse))


def mirror_tables(rows, length):
    part = length // 2
    m = np.arange(part)
    order = np.concatenate([2 * m, 2 * m + 1])
    straight = np.zeros((length, length))
    straight[order, np.arange(length)] = 1.0
    mirrored = np.zeros((length, length))
    mirrored[(length - order) % length, np.arange(length)] = 1.0
    flip = np.zeros((rows, rows))
    i = np.arange(1, rows)
    flip[i, rows - i] = 1.0
    as_bf16 = lambda table: table.astype(ml_dtypes.bfloat16)
    return as_bf16(straight), as_bf16(mirrored), as_bf16(flip)


def halves(values):
    high = values.astype(BF16)
    return high, (values - high.astype(F32)).astype(BF16)


def dot(a, b):
    return jnp.dot(a, b, preferred_element_type=F32)


def table_first(high, low, values):
    top, rest = halves(values)
    width = values.shape[1]
    if width % LANES == 0:
        both = dot(high, jnp.concatenate([top, rest], axis=1))
        both = both[:, :width] + both[:, width:]
    else:
        both = dot(high, top) + dot(high, rest)
    return both + dot(low, top)


def table_last(values, high, low):
    top, rest = halves(values)
    rows = values.shape[0]
    both = dot(jnp.concatenate([top, rest], axis=0), high)
    return both[:rows] + both[rows:] + dot(top, low)


def cost(*arrays):
    size = sum(math.prod(array.shape) * 4 for array in arrays)
    return pl.CostEstimate(flops=0, bytes_accessed=5 * size, transcendentals=0)


def complex_last(values, high, low, back):
    middle = values.shape[1] // 2
    re, im = values[:, :middle], values[:, middle:]
    both = table_last(re + im, high[0], low[0])
    if back:
        pair = both - table_last(im, high[2], low[2]), both + table_last(re, high[1], low[1])
    else:
        pair = both + table_last(im, high[1], low[1]), both - table_last(re, high[2], low[2])
    return jnp.concatenate(pair, axis=1)


def params(mib):
    return pltpu.CompilerParams(vmem_limit_bytes=mib * MIB)


ANYWHERE = pl.BlockSpec(memory_space=pl.ANY)


def waiting(kernel, before, after):
    def body(*refs):
        kernel(*refs[:before], *refs[before + len(after) :])

    return body


def whole(array):
    rank = len(array.shape)
    return pl.BlockSpec(array.shape, lambda *_: (0,) * rank)


def depth_kernel(weights, place, eta, high, low, out):
    boxes, extent, span = eta.shape[0], eta.shape[1], eta.shape[2]
    owners = out.shape[0]
    planes = high.shape[0] // owners
    dims = (((1,), (1,)), ((), ()))
    for i in range(extent):
        rows = []
        for b in range(boxes):
            values = eta[b, i]
            rows.append(weights[b] * (values * values))
        field = jnp.concatenate(rows, axis=0)
        top, rest = halves(field)
        count = field.shape[0]
        both = lax.dot_general(
            high[...], jnp.concatenate([top, rest], axis=0), dims, preferred_element_type=F32
        )
        small = lax.dot_general(low[...], top, dims, preferred_element_type=F32)
        result = both[:, :count] + both[:, count:] + small
        for p in range(owners):
            out[p, pl.ds(i, planes, stride=extent), :] = result[p * planes : (p + 1) * planes]
    lane = lax.broadcasted_iota(jnp.int32, (STEP, boxes * span), 1)
    where_to = jnp.zeros(lane.shape, jnp.int32)
    for k in range(2 * boxes):
        where_to = jnp.where(lane == k, place[k], where_to)
    for p in range(owners):
        out[p, planes * extent :, :] = where_to.astype(F32)


def box_depth(eta_boxes, weights, place, tables, owners, after):
    high, low = tables
    boxes, extent, span, depth = eta_boxes.shape
    shape = (owners, high.shape[0] // owners * extent + STEP, boxes * span)
    return pl.pallas_call(
        waiting(depth_kernel, 5, after),
        out_shape=jax.ShapeDtypeStruct(shape, F32),
        in_specs=[
            pl.BlockSpec(memory_space=pltpu.SMEM),
            pl.BlockSpec(memory_space=pltpu.SMEM),
            whole(eta_boxes),
            whole(high),
            whole(low),
            *([ANYWHERE] * len(after)),
        ],
        out_specs=pl.BlockSpec(shape, lambda: (0, 0, 0)),
        compiler_params=params(24),
        cost_estimate=cost(eta_boxes, eta_boxes),
        name="box_depth",
    )(weights, place, eta_boxes, high, low, *after)


def rows_kernel(shape, place, boxes_re, boxes_im, high, low, out, lines, packed):
    owners, per_owner, half, extent, span, length, cols, over, slots, packs = shape
    step = pl.program_id(0)
    lane = lax.broadcasted_iota(jnp.int32, (extent, LANES), 1)
    side = lines.shape[0]

    @pl.when(step == 0)
    def _():
        packed[...] = jnp.zeros(packed.shape, F32)

    @pl.when((step <= half) & (step != 1))
    def _():
        lines[...] = jnp.zeros(lines.shape, F32)

        def add_owner(s, carry):
            values = (boxes_re[s], boxes_im[s])
            moved = []
            for b in range(per_owner):
                column = place[2 * (s * per_owner + b) + 1]
                inside = (lane >= b * span) & (lane < (b + 1) * span)
                shift = lax.rem(column + (LANES - b * span), LANES)
                for v in values:
                    moved.append(pltpu.roll(jnp.where(inside, v, 0.0), shift, axis=1))
            for b in range(per_owner):
                at = 2 * (s * per_owner + b)
                where_to = pl.ds(pl.multiple_of(place[at], STEP), extent)
                here = lane >= place[at + 1]
                for ri in range(2):
                    value = moved[2 * b + ri]
                    lines[0, ri, where_to, :] += jnp.where(here, value, 0.0)
                    if side > 1:
                        lines[1, ri, where_to, :] += jnp.where(here, 0.0, value)
            return carry

        lax.fori_loop(0, owners, add_owner, 0, unroll=4)
        lines[:, :, :extent, :] += lines[:, :, length:, :]

    sign = jnp.where(step == 1, -1.0, 1.0).astype(F32)

    for k in range(half + 1):
        slot = half if k == 1 else max(k - 1, 0)

        @pl.when(step == k)
        def _(slot=slot):
            lanes_all = lax.broadcasted_iota(jnp.int32, (length, LANES), 1)
            for ri in range(2):
                beyond = lines[side - 1, ri, :length, :]
                if side == 1:
                    beyond = jnp.where(lanes_all >= cols, beyond, 0.0)
                shift = ((slot % slots) * over - (cols % LANES)) % LANES
                if shift:
                    beyond = pltpu.roll(beyond, shift, axis=1)
                packed[slot // slots, ri] += beyond * (sign if ri else 1.0)

    for k in range(packs):

        @pl.when(step == half + 1 + k)
        def _(k=k):
            lines[0, :, :length, :] = packed[k]

    part = length // RADIX
    terms = []
    for l in range(RADIX):
        take = pl.ds(l, part, stride=RADIX)
        re, im = lines[0, 0, take, :], lines[0, 1, take, :] * sign
        both = table_first(high[l, 0], low[l, 0], re + im)
        terms.append(
            (
                both + table_first(high[l, 1], low[l, 1], im),
                both - table_first(high[l, 2], low[l, 2], re),
            )
        )
    real, imag = [v[0] for v in terms], [v[1] for v in terms]
    root = math.sqrt(0.75)
    sum_re, sum_im = real[1] + real[2], imag[1] + imag[2]
    dif_re, dif_im = root * (real[1] - real[2]), root * (imag[1] - imag[2])
    mid_re, mid_im = real[0] - 0.5 * sum_re, imag[0] - 0.5 * sum_im
    result_re = jnp.concatenate([real[0] + sum_re, mid_re + dif_im, mid_re - dif_im], axis=0)
    result_im = jnp.concatenate([imag[0] + sum_im, mid_im - dif_re, mid_im + dif_re], axis=0)
    block = (out.shape[0], out.shape[3], LANES)
    out[:, 0, 0] = result_re.reshape(block)[:, :, :cols]
    out[:, 1, 0] = result_im.reshape(block)[:, :, :cols]


def box_rows(pieces, place, tables, shape, parts, after):
    owners, per_owner, half, extent, span, length, cols, over, slots, packs = shape
    high, low = tables
    planes = half + 1 + packs
    rows = length // parts
    side = -(-(cols + over) // LANES)

    def plane_in(k):
        return jnp.clip(k - 1, 0, half - 1)

    def plane_out(k, place):
        return (0, 0, jnp.where(k == 1, half, jnp.where(k > half, k, jnp.maximum(k - 1, 0))), 0, 0)

    return pl.pallas_call(
        waiting(functools.partial(rows_kernel, shape), 5, after),
        out_shape=jax.ShapeDtypeStruct((parts, 2, planes, rows, cols), F32),
        grid_spec=pltpu.PrefetchScalarGridSpec(
            num_scalar_prefetch=1,
            grid=(planes,),
            in_specs=[
                pl.BlockSpec((owners, extent, LANES), lambda k, place: (0, plane_in(k), 0)),
                pl.BlockSpec((owners, extent, LANES), lambda k, place: (0, half + plane_in(k), 0)),
                whole(high),
                whole(low),
                *([ANYWHERE] * len(after)),
            ],
            out_specs=pl.BlockSpec((parts, 2, 1, rows, cols), plane_out),
            scratch_shapes=[
                pltpu.VMEM((side, 2, length + extent, LANES), F32),
                pltpu.VMEM((packs, 2, length, LANES), F32),
            ],
        ),
        compiler_params=params(56),
        cost_estimate=cost(pieces, jax.ShapeDtypeStruct((parts, 2, planes, rows, cols), F32)),
        name="box_rows",
    )(place, pieces, pieces, high, low, *after)


def columns_kernel(slots, over, has_packs, has_conj, begin, half, counts, *refs):
    refs = list(refs)
    me = refs.pop(0)[0]
    main = refs.pop(0)
    pack = refs.pop(0) if has_packs else None
    conj = refs.pop(0) if has_conj else None
    conj_pack = refs.pop(0) if has_conj and has_packs else None
    own = refs.pop(0)
    mirrors = [refs.pop(0) for _ in counts]
    first_gain, conj_gain = (refs.pop(0), refs.pop(0)) if has_conj else (None, None)
    fwd_high, fwd_low, inv_high, inv_low = refs[:4]
    parts = main.shape[0]
    outs = refs[-2 - parts : -2]
    scratch, lines = refs[-2:]
    step = pl.program_id(0)
    rows, cols = main.shape[3], main.shape[4]
    half_length = fwd_high.shape[2]

    def gathered(body, overhang, slot):
        pieces = []
        for ri in range(2):
            line = []
            for q in range(parts):
                piece = body[q, ri, 0]
                if has_packs:
                    lane = lax.broadcasted_iota(jnp.int32, piece.shape, 1)
                    shift = lax.rem(cols - over * slot, cols)
                    beyond = pltpu.roll(overhang[(q - 1) % parts, ri, 0], shift, axis=1)
                    piece = piece + jnp.where(lane < over, beyond, 0.0)
                line.append(piece)
            pieces.append(jnp.concatenate(line, axis=1) if parts > 1 else line[0])
        lower = [v[:, :half_length] for v in pieces]
        upper = [v[:, half_length:] for v in pieces]
        even = jnp.concatenate([a + b for a, b in zip(lower, upper)], axis=1)
        odd = jnp.concatenate([a - b for a, b in zip(lower, upper)], axis=1)
        return even, odd

    def forward(body, overhang, slot):
        even, odd = gathered(body, overhang, slot)
        return (
            complex_last(even, fwd_high[0], fwd_low[0], False),
            complex_last(odd, fwd_high[1], fwd_low[1], False),
        )

    def scaled(spectrum, gain):
        even, odd = spectrum
        left, right = gain[:, :half_length], gain[:, half_length:]
        left = jnp.concatenate([left, left], axis=1)
        right = jnp.concatenate([right, right], axis=1)
        return even * left, odd * right

    mirror = mirrors[0][0]
    for k in range(1, len(counts)):
        mirror = jnp.where(step >= sum(counts[:k]), mirrors[k][0], mirror)
    gain = own[0] + mirror
    if has_conj:
        gain = jnp.where(step == 0, first_gain[...], gain)
    even, odd = scaled(forward(main, pack, lax.rem(step + begin, slots)), gain)
    scratch[0] = even
    scratch[1] = odd

    if has_conj:

        @pl.when(step == 0)
        def _():
            even, odd = scaled(forward(conj, conj_pack, half % slots), conj_gain[...])
            scratch[0] += even
            scratch[1] += odd

    even = complex_last(scratch[0], inv_high[0], inv_low[0], True)
    odd = complex_last(scratch[1], inv_high[1], inv_low[1], True)
    lower, upper = even + odd, even - odd
    for ri in range(2):
        take = slice(ri * half_length, (ri + 1) * half_length)
        line = jnp.concatenate([lower[:, take], upper[:, take]], axis=1)
        for q in range(parts):
            lines[q] = line[:, q * cols : (q + 1) * cols]
        for r, out in enumerate(outs):
            out[ri, 0] = lines[lax.rem(me + r, parts)]


def grid_columns(me, arrived, count, half, own, begin, mirror, gains, forward, inverse, slots, over, packs, after):
    parts, _, planes, rows, cols = arrived.shape
    length = own.shape[2]
    has_packs, has_conj = packs > 0, gains is not None
    one = (parts, 2, 1, rows, cols)
    operands = [me, arrived]
    specs = [
        pl.BlockSpec(memory_space=pltpu.SMEM),
        pl.BlockSpec(one, lambda t: (0, 0, begin + t, 0, 0)),
    ]
    if has_packs:
        operands += [arrived]
        specs += [pl.BlockSpec(one, lambda t: (0, 0, half + 1 + (begin + t) // slots, 0, 0))]
    if has_conj:
        operands += [arrived]
        specs += [pl.BlockSpec(one, lambda t: (0, 0, half, 0, 0))]
        if has_packs:
            operands += [arrived]
            specs += [pl.BlockSpec(one, lambda t: (0, 0, half + 1 + half // slots, 0, 0))]
    operands += [own, *mirror]
    specs += [pl.BlockSpec((1, rows, length), lambda t: (begin + t, 0, 0))]
    counts = [m.shape[0] for m in mirror]
    for k, many in enumerate(counts):
        skip = sum(counts[:k])
        specs += [
            pl.BlockSpec(
                (1, rows, length),
                lambda t, skip=skip, many=many: (jnp.clip(t - skip, 0, many - 1), 0, 0),
            )
        ]
    fixed = [*(gains or ()), *forward, *inverse]
    return pl.pallas_call(
        functools.partial(columns_kernel, slots, over, has_packs, has_conj, begin, half, counts),
        out_shape=[jax.ShapeDtypeStruct((2, count, rows, cols), F32)] * parts,
        grid=(count,),
        in_specs=specs + [whole(t) for t in fixed] + [ANYWHERE] * len(after),
        out_specs=[pl.BlockSpec((2, 1, rows, cols), lambda t: (0, t, 0, 0))] * parts,
        scratch_shapes=[
            pltpu.VMEM((2, rows, length), F32),
            pltpu.VMEM((parts, rows, cols), F32),
        ],
        compiler_params=params(56),
        cost_estimate=cost(jax.ShapeDtypeStruct((parts, 6, count, rows, cols), F32)),
        name="grid_columns",
    )(*operands, *fixed, *after)


def back_rows_kernel(count, *refs):
    me = refs[0][0]
    bodies = refs[1 : 1 + count]
    high, low, out, lines = refs[1 + count :]
    parts, rows, cols = lines.shape[0], lines.shape[2], lines.shape[3]
    length = parts * rows
    part = length // RADIX
    owners, group = out.shape[0], out.shape[3] // RADIX
    if count == 1:
        lines[...] = bodies[0][:, :, 0]
    else:
        for r, body in enumerate(bodies):
            lines[lax.rem(me - r + parts, parts)] = body[:, 0]
    real = lines[:, 0].reshape(length, cols)
    imag = lines[:, 1].reshape(length, cols)
    real = [real[t * part : (t + 1) * part] for t in range(RADIX)]
    imag = [imag[t * part : (t + 1) * part] for t in range(RADIX)]
    root = math.sqrt(0.75)
    sum_re, sum_im = real[1] + real[2], imag[1] + imag[2]
    dif_re, dif_im = root * (real[1] - real[2]), root * (imag[1] - imag[2])
    mid_re, mid_im = real[0] - 0.5 * sum_re, imag[0] - 0.5 * sum_im
    terms = [
        (real[0] + sum_re, imag[0] + sum_im),
        (mid_re - dif_im, mid_im + dif_re),
        (mid_re + dif_im, mid_im - dif_re),
    ]
    for l in range(RADIX):
        re, im = terms[l]
        both = table_first(high[l, 0], low[l, 0], re + im)
        result = (
            both - table_first(high[l, 2], low[l, 2], im),
            both + table_first(high[l, 1], low[l, 1], re),
        )
        for ri in range(2):
            values = result[ri].reshape(owners, group, cols)
            out[:, ri, 0, l * group : (l + 1) * group, :] = values


def back_rows(me, bodies, tables, owners, after):
    high, low = tables
    half, rows, cols = bodies[0].shape[-3:]
    if len(bodies) == 1:
        parts = bodies[0].shape[0]
        spec = pl.BlockSpec((parts, 2, 1, rows, cols), lambda t: (0, 0, t, 0, 0))
    else:
        parts = len(bodies)
        spec = pl.BlockSpec((2, 1, rows, cols), lambda t: (0, t, 0, 0))
    length = parts * rows
    out = jax.ShapeDtypeStruct((owners, 2, half, length // owners, cols), F32)
    return pl.pallas_call(
        waiting(functools.partial(back_rows_kernel, len(bodies)), len(bodies) + 3, after),
        out_shape=out,
        grid=(half,),
        in_specs=[pl.BlockSpec(memory_space=pltpu.SMEM)]
        + [spec] * len(bodies)
        + [whole(high), whole(low)]
        + [ANYWHERE] * len(after),
        out_specs=pl.BlockSpec((owners, 2, 1, length // owners, cols), lambda t: (0, 0, t, 0, 0)),
        scratch_shapes=[pltpu.VMEM((parts, 2, rows, cols), F32)],
        compiler_params=params(56),
        cost_estimate=cost(out, out),
        name="back_rows",
    )(me, *bodies, high, low, *after)


def back_depth_kernel(chunks, *refs):
    bodies = refs[:chunks]
    high, low = refs[chunks : chunks + 2]
    out = refs[-1]
    group = out.shape[0]
    dims = (((0,), (0,)), ((), ()))
    for g in range(group):
        for l in range(RADIX):
            lines = [body[:, l, g, :] for body in bodies]
            values = jnp.concatenate(lines, axis=0) if chunks > 1 else lines[0]
            top, rest = halves(values)
            total = lax.dot_general(top, high[...], dims, preferred_element_type=F32)
            total += lax.dot_general(rest, high[...], dims, preferred_element_type=F32)
            total += lax.dot_general(top, low[...], dims, preferred_element_type=F32)
            out[g, l] = total


def back_depth(arrived, tables, after, only=None):
    high, low = tables
    chunks = len(arrived)
    depth = high.shape[1]
    rows, cols = arrived[0].shape[-2:]
    group = rows // RADIX
    take = group if only is None else only // RADIX
    bodies = [piece.reshape(-1, RADIX, group, cols) for piece in arrived]
    blocks = [(body.shape[0], RADIX, STEP, cols) for body in bodies]
    found = pl.pallas_call(
        functools.partial(back_depth_kernel, chunks),
        out_shape=jax.ShapeDtypeStruct((take, RADIX, cols, depth), F32),
        grid=(take // STEP,),
        in_specs=[pl.BlockSpec(block, lambda g: (0, 0, g, 0)) for block in blocks]
        + [whole(high), whole(low)]
        + [ANYWHERE] * len(after),
        out_specs=pl.BlockSpec((STEP, RADIX, cols, depth), lambda g: (g, 0, 0, 0)),
        compiler_params=params(56),
        cost_estimate=cost(*bodies, *bodies),
        name="back_depth",
    )(*bodies, high, low, *after)
    return found.reshape(take * RADIX, cols, depth)


def mirror_kernel(index, other, edge, mirrored, flip, out):
    rows, length = other.shape[1], other.shape[2]
    top, rest = halves(other[0])
    turned = dot(flip[...], jnp.concatenate([top, rest], axis=1))
    edge_top, edge_rest = halves(edge[0])
    row = lax.broadcasted_iota(jnp.int32, (rows, length), 0)
    top = jnp.where(row == 0, edge_top.astype(F32), turned[:, :length])
    rest = jnp.where(row == 0, edge_rest.astype(F32), turned[:, length:])
    both = dot(jnp.concatenate([top, rest], axis=0).astype(BF16), mirrored[...])
    out[0] = both[:rows] + both[rows:]


def mirror_planes(green, edge, index, mirrored, flip, after):
    rows, length = green.shape[1:]
    block = (1, rows, length)
    count = index.shape[0]
    return pl.pallas_call(
        waiting(mirror_kernel, 5, after),
        out_shape=jax.ShapeDtypeStruct((count, rows, length), F32),
        grid_spec=pltpu.PrefetchScalarGridSpec(
            num_scalar_prefetch=1,
            grid=(count,),
            in_specs=[
                pl.BlockSpec(block, lambda t, index: (index[t], 0, 0)),
                pl.BlockSpec((1, 1, length), lambda t, index: (index[t], 0, 0)),
                whole(mirrored),
                whole(flip),
                *([ANYWHERE] * len(after)),
            ],
            out_specs=pl.BlockSpec(block, lambda t, index: (t, 0, 0)),
        ),
        compiler_params=params(16),
        cost_estimate=cost(jax.ShapeDtypeStruct((count, rows, length), F32)),
        name="mirror_planes",
    )(index, green, edge, mirrored, flip, *after)


def order_kernel(index, own, straight, out):
    rows = own.shape[1]
    top, rest = halves(own[0])
    both = dot(jnp.concatenate([top, rest], axis=0), straight[...])
    out[0] = both[:rows] + both[rows:]


def order_planes(green, index, straight, after):
    rows, length = green.shape[1:]
    block = (1, rows, length)
    count = index.shape[0]
    return pl.pallas_call(
        waiting(order_kernel, 3, after),
        out_shape=jax.ShapeDtypeStruct((count, rows, length), F32),
        grid_spec=pltpu.PrefetchScalarGridSpec(
            num_scalar_prefetch=1,
            grid=(count,),
            in_specs=[
                pl.BlockSpec(block, lambda t, index: (index[t], 0, 0)),
                whole(straight),
                *([ANYWHERE] * len(after)),
            ],
            out_specs=pl.BlockSpec(block, lambda t, index: (t, 0, 0)),
        ),
        compiler_params=params(16),
        cost_estimate=cost(jax.ShapeDtypeStruct((count, rows, length), F32)),
        name="order_planes",
    )(index, green, straight, *after)


def edges_of(body, axis, first, last):
    over = first.shape[axis]
    if axis == 0:
        first[...] = body[:over]
        last[...] = body[body.shape[0] - over :]
    else:
        first[...] = body[:, :over, :]
        last[...] = body[:, body.shape[1] - over :, :]


def patch_kernel(place, eta, out, first, last):
    boxes, extent, span = eta.shape[0], eta.shape[1], eta.shape[2]
    out[...] = jnp.zeros(out.shape, F32)
    for b in range(boxes):
        row = place[2 * b]
        columns = pl.ds(pl.multiple_of(place[2 * b + 1], STEP), span)

        def add_row(i, carry, b=b, row=row, columns=columns):
            values = eta[b, i]
            out[row + i, columns, :] += values * values
            return carry

        lax.fori_loop(0, extent, add_row, 0, unroll=4)
    edges_of(out, 0, first, last)


def occupancy_patch(eta_boxes, place, rows, cols, over, after):
    depth = eta_boxes.shape[3]
    shapes = [(rows, cols, depth), (over, cols, depth), (over, cols, depth)]
    return pl.pallas_call(
        waiting(patch_kernel, 2, after),
        out_shape=[jax.ShapeDtypeStruct(shape, F32) for shape in shapes],
        in_specs=[pl.BlockSpec(memory_space=pltpu.SMEM), whole(eta_boxes)]
        + [ANYWHERE] * len(after),
        out_specs=[pl.BlockSpec(shape, lambda: (0, 0, 0)) for shape in shapes],
        compiler_params=params(32),
        cost_estimate=cost(eta_boxes),
        name="occupancy_patch",
    )(place, eta_boxes, *after)


def join_rows_kernel(body, behind, ahead, out, first, last):
    step, steps = pl.program_id(0), pl.num_programs(0)
    near = behind.shape[0] // out.shape[0]
    out[...] = body[...]
    count = out.shape[0]

    @pl.when(step < near)
    def _():
        out[...] += behind[pl.ds(step * count, count)]

    @pl.when(step >= steps - near)
    def _():
        out[...] += ahead[pl.ds((step - steps + near) * count, count)]

    edges_of(out, 1, first, last)


def join_rows(patch, behind, ahead, over, after):
    rows, cols, depth = patch.shape
    spec = pl.BlockSpec((STEP, cols, depth), lambda r: (r, 0, 0))
    side = pl.BlockSpec((STEP, over, depth), lambda r: (r, 0, 0))
    edge = jax.ShapeDtypeStruct((rows, over, depth), F32)
    return pl.pallas_call(
        waiting(join_rows_kernel, 3, after),
        out_shape=[jax.ShapeDtypeStruct(patch.shape, F32), edge, edge],
        grid=(rows // STEP,),
        in_specs=[spec, whole(behind), whole(ahead)] + [ANYWHERE] * len(after),
        out_specs=[spec, side, side],
        compiler_params=params(24),
        cost_estimate=cost(patch),
        name="join_rows",
    )(patch, behind, ahead, *after)


def apply_kernel(inside, place, weights, base, eta, *refs):
    sources, out = refs[:-1], refs[-1]
    boxes, extent, span = eta.shape[0], eta.shape[1], eta.shape[2]
    rows, cols = inside
    out[...] = base[...]

    def one_box(b, carry):
        first, column = place[2 * b], place[2 * b + 1]
        factor = (-2.0 * rate_step) * weights[b]
        for i in range(0, extent, STEP):
            x = first + i
            for j in range(0, span, STEP):
                y = pl.multiple_of(column + j, STEP)
                places = [
                    ((x < rows) & (y < cols), x, y),
                    ((x < rows) & (y >= cols), x, y - cols),
                    ((x >= rows) & (y < cols), x - rows, y),
                    ((x >= rows) & (y >= cols), x - rows, y - cols),
                ]
                places = places[:1] if len(sources) == 1 else places[1:]
                for source, (take, at_x, at_y) in zip(sources, places):

                    @pl.when(take)
                    def _(source=source, i=i, j=j, at_x=at_x, at_y=pl.multiple_of(at_y, STEP)):
                        mu = source[pl.ds(at_x, STEP), pl.ds(at_y, STEP), :]
                        here = (b, pl.ds(i, STEP), pl.ds(j, STEP), slice(None))
                        out[here] += factor * eta[here] * mu

        return carry

    lax.fori_loop(0, boxes, one_box, 0)


def apply_potential(place, weights, base, eta_boxes, sources, inside):
    arrays = [base, eta_boxes, *sources]
    smem = pl.BlockSpec(memory_space=pltpu.SMEM)
    return pl.pallas_call(
        functools.partial(apply_kernel, inside),
        out_shape=jax.ShapeDtypeStruct(eta_boxes.shape, F32),
        in_specs=[smem, smem] + [whole(v) for v in arrays],
        out_specs=whole(eta_boxes),
        compiler_params=params(36),
        cost_estimate=cost(eta_boxes, eta_boxes),
        name="apply_potential",
    )(place, weights, *arrays)


def halved(count):
    return [count // 2, count - count // 2] if count > 1 else [1]


def exchange(shard, axis):
    return lax.all_to_all(shard, axis, split_axis=0, concat_axis=0, tiled=True)


def send_round(lines, axis):
    return [lines[0]] + [from_behind(lines[r], axis, r) for r in range(1, len(lines))]


def potential_pieces(field, rows, over_x, over_y):
    px, py = lax.axis_size("px"), lax.axis_size("py")
    below = from_behind(rows, "px", -1)
    right = from_behind(field[:, :over_y], "py", -1)
    pairs = [
        (a * py + b, ((a - 1) % px) * py + (b - 1) % py) for a in range(px) for b in range(py)
    ]
    corner = lax.ppermute(rows[:, :over_y], ("px", "py"), pairs)
    return right, below, corner


def without_packs(along_x, count, slots, over, parts):
    body = count
    shifted = jnp.roll(along_x[:, :, body:], 1, axis=0)
    pieces = []
    for k in range(body):
        at = (k % slots) * over
        pieces.append(shifted[:, :, k // slots, :, at : at + over])
    body = along_x[:, :, :body].at[..., :over].add(jnp.stack(pieces, axis=2))
    body = jnp.transpose(body, (1, 2, 3, 0, 4))
    return body.reshape((1,) + body.shape[:3] + (-1,))


def on_device(eta_boxes, corners, grain_ids, misfit, green):
    px, py = lax.axis_size("px"), lax.axis_size("py")
    p = lax.axis_index("px")
    middle = px // 2
    box_count, extent, span, depth = eta_boxes.shape
    own, kx_rows, length_y = green.shape
    length_x = kx_rows * py
    rows_dev, cols_dev = length_x // px, length_y // py
    over_x, over_y = extent - STEP, span - STEP
    half = own // 2
    sizes = halved(half)
    begins = [sum(sizes[:k]) for k in range(len(sizes))]
    pieces = [halved(sizes[0]), *([size] for size in sizes[1:])]
    slots = cols_dev // over_y
    first_x = corners[:, 0] * STEP
    start_x = first_x - p * rows_dev
    start_y = corners[:, 1] * STEP - lax.axis_index("py") * cols_dev
    place_here = jnp.stack([start_x, start_y], axis=1).reshape(-1)
    variant = jnp.arange(misfit.shape[0], dtype=jnp.int32)
    weights = jnp.sum(
        jnp.where(grain_ids[:, None] == variant[None, :], misfit[None, :], 0.0), axis=1
    )
    scale = 1.0 / (length_x * length_y * depth)
    depth_forward, depth_inverse = depth_tables(depth, px, sizes, scale)
    rows_forward, rows_inverse = row_tables(length_x)
    cols_forward, cols_inverse = column_tables(length_y)
    straight, mirrored, flip = mirror_tables(kx_rows, length_y)

    edge = from_behind(green[:, :1, :], "py", -1)
    place_send = jnp.stack([first_x, start_y], axis=1).reshape(-1)
    spectra = box_depth(eta_boxes, weights, place_send, depth_forward, px, ())
    arrived = exchange(spectra, "px")
    place = arrived[:, -STEP, : 2 * box_count].astype(jnp.int32).reshape(-1)

    lower = (p < middle).astype(jnp.int32)
    t = jnp.arange(half, dtype=jnp.int32)
    facing = [(i, py - 1 - i) for i in range(py)]
    zero_index = jnp.zeros((1,), jnp.int32)
    index = jnp.minimum(own - 1 - t + lower, own - 1)
    indices = jnp.split(index, np.cumsum(sum(pieces, []))[:-1].tolist())
    indices[0] = jnp.concatenate([zero_index, indices[0]])
    own_zero = order_planes(green, zero_index, straight, (spectra,))
    mirror = [own_zero]
    for which in indices:
        mirror.append(mirror_planes(green, edge, which, mirrored, flip, (mirror[-1],)))
    own_planes = order_planes(green, t + lower, straight, (mirror[-1],))
    patch, first, last = occupancy_patch(
        eta_boxes, place_here, rows_dev + over_x, cols_dev + over_y, over_x, (own_planes,)
    )
    first_leg = [lax.ppermute(planes, "py", facing) for planes in mirror[1:]]
    mirror_zero, first_leg[0] = first_leg[0][:1], first_leg[0][1:]
    middle_own = 0.5 * (own_zero + mirror_zero)
    payload = jnp.where(p == 0, middle_own, mirror_zero)
    pairs = [(0, middle)] + [(i, px - i) for i in range(1, middle)]
    from_zero = lax.ppermute(payload, "px", pairs)

    opposite = [(i, px - 1 - i) for i in range(px)]
    mirror = [lax.ppermute(planes, "px", opposite) for planes in first_leg]
    packs = -(-(half + 1) // slots)
    shape = (px, box_count, half, extent, span, length_x, cols_dev, over_y, slots, packs)
    after = (patch, from_zero, *first_leg, mirror[0])
    lines = box_rows(arrived, place, rows_forward, shape, py, after)
    along_x = exchange(lines, "py")
    first, last = from_behind(last, "px", 1), from_behind(first, "px", -1)
    mirror = [mirror[: len(pieces[0])], *([m] for m in mirror[len(pieces[0]) :])]
    first_gain = own_planes[:1] + jnp.where(p < middle, mirror[0][0][:1], from_zero)
    first_gain = jnp.where(p == middle, middle_own + from_zero, first_gain)
    conj_gain = jnp.where(p == middle, middle_own - from_zero, 0.0)
    gains = (first_gain[0], conj_gain[0])

    if cols_dev % LANES:
        along_x, packs = without_packs(along_x, half + 1, slots, over_y, py), 0
    me = lax.axis_index("py").astype(jnp.int32).reshape(1)
    arrays = []
    for k, size in enumerate(sizes):
        lines = grid_columns(
            me,
            along_x,
            size,
            half,
            own_planes,
            begins[k],
            mirror[k],
            gains if k == 0 else None,
            cols_forward,
            cols_inverse,
            slots,
            over_y,
            packs,
            (lines,) if k else (),
        )
        back = lines[0]
        if cols_dev % LANES:
            lines = lines[0].reshape(2, size, kx_rows, py, cols_dev)
            lines = [exchange(jnp.transpose(lines, (3, 0, 1, 2, 4)), "py")]
        else:
            lines = send_round(lines, "py")
        if k == 0:
            patch, first, last = join_rows(patch, first, last, over_y, (back,))
        lines = back_rows(me, lines, rows_inverse, px, () if k else (patch, *sum(mirror, [])))
        arrays.append(exchange(lines, "px"))
    first, last = from_behind(last, "py", 1), from_behind(first, "py", -1)

    window = patch.at[:, :over_y].add(first).at[:, cols_dev:].add(last)
    zero = jnp.zeros((), jnp.int32)
    results = []
    for b in range(box_count):
        position = (start_x[b], start_y[b], zero)
        total = lax.dynamic_slice(window, position, eta_boxes.shape[1:])
        results.append(advance(eta_boxes[b], total))
    base = jnp.stack(results)

    rows = back_depth(arrays, depth_inverse, (base,), over_x)
    potential = back_depth(arrays, depth_inverse, (rows,))
    pieces = potential_pieces(potential, rows, over_x, over_y)
    inside = (rows_dev, cols_dev)
    base = apply_potential(place_here, weights, base, eta_boxes, [potential], inside)
    return (apply_potential(place_here, weights, base, eta_boxes, pieces, inside), potential)


def solution(mesh):
    in_specs = (
        P(("px", "py"), None, None, None),
        P(("px", "py"), None),
        P(("px", "py")),
        P(),
        P("px", "py", None),
    )
    out_specs = (P(("px", "py"), None, None, None), P("px", "py", None))
    return jax.shard_map(
        on_device, mesh=mesh, in_specs=in_specs, out_specs=out_specs, check_vma=False
    )
```
